512 devices in a mesh: stream: 32 (over z_hi, y, core), azi: 16 (over z_lo, x).
Axes of the slice: x: 4, y: 8, z: 8 (z_hi: 2, z_lo: 4; z = z_hi * 4 + z_lo), core: 2. Of those that a mesh axis runs over, the one named last changes fastest.
Arguments:
- velocity: float32 [3, 64, 256, 2048], P(None, 'stream', None, 'azi'), may hold values from -6 to 6
- mean_flow: float32 [256], replicated, may hold values from 0.5 to 1.5
- part_x: int32 [32, 16, 16, 128], P('stream', 'azi'), may hold values from 0 to 1
- part_r: int32 [32, 16, 16, 128], P('stream', 'azi'), may hold values from 0 to 255
- part_t: int32 [32, 16, 16, 128], P('stream', 'azi'), may hold values from 0 to 127
- part_vel: float32 [32, 16, 16, 3, 128], P('stream', 'azi'), may hold values from -6 to 6
- part_rate: float32 [32, 16, 16, 128], P('stream', 'azi'), may hold values from 0.5 to 5
- counts: int32 [32, 16, 16], P('stream', 'azi'), may hold values from 1 to 128, as said below
Outputs:
- new_velocity: float32 [3, 64, 256, 2048], P(None, 'stream', None, 'azi')
- new_part_vel: float32 [32, 16, 16, 3, 128], P('stream', 'azi')
The draws below stay inside these ranges and needn't reach their ends.
Inputs may be any that keep to these rules, and one draw needn't show every extreme that they name: `counts`: in every source slab and source device, at least one block is full (128 live); in each streamwise group some owner receives a full block from every source device.
All inputs are finite; a program needn't handle non-finite values.
Results may differ from the reference program's by a relative error of at most 0.00002.
Values sent between devices are 32-bit elements; how exact they have to be, the bound alone decides.
A program may use at most 128 MiB of HBM per device.

```python
import math
import jax
import jax.numpy as jnp

CX = 2
CR = 256
CT = 128
CAP = 128
NX = 64
NR = 256
NT = 2048
N_STREAM = 32
N_AZI = 16


def draw_counts(key, part):
    key = jax.random.fold_in(key, 11)
    first, second, third = jax.random.split(key, 3)
    base = jax.random.randint(first, (N_STREAM, N_AZI, N_AZI), 1, CAP + 1)
    hottest = jax.random.randint(second, (N_STREAM, 1, 1), 0, N_AZI)
    fullest = jax.random.randint(third, (N_STREAM, N_AZI, 1), 0, N_AZI)
    owners = jnp.arange(N_AZI, dtype=jnp.int32)[None, None, :]
    chosen = jnp.logical_or(owners == hottest, owners == fullest)
    return jnp.where(chosen, CAP, base).astype(jnp.int32)


def with_ends(drawn, key, least, high):
    index_at = [jax.random.randint(jax.random.fold_in(key, axis), (), 0, length) for axis, length in enumerate(drawn.shape)]
    longest = drawn.shape.index(max(drawn.shape))
    neighbour = index_at[:longest] + [(index_at[longest] + 1) % drawn.shape[longest]] + index_at[longest + 1:]
    return drawn.at[tuple(index_at)].set(least).at[tuple(neighbour)].set(high)


def shard_levels(own_key, extent, cuts, smallest, largest):
    level, own = 1.0, jax.random.fold_in(own_key, 6)
    for axis_at, shards_of in cuts:
        steps = jnp.exp(jax.random.uniform(jax.random.fold_in(own, axis_at), (shards_of,), jnp.float32, smallest / len(cuts), largest / len(cuts)))
        level = level * jnp.repeat(steps, extent[axis_at] // shards_of).reshape([-1 if axis == axis_at else 1 for axis in range(len(extent))])
    return level


def centred(rng, dims, spread, most, pieces=(), held_as=jnp.bfloat16):
    array = jax.random.normal(rng, dims, jnp.float32) * spread
    if len(pieces) > 0:
        array = shard_levels(rng, dims, pieces, -0.22, 0.18) * array
    return jnp.clip(array, min=-most, max=most).astype(held_as)


def setup_inputs(seed: int = 0) -> dict:
    arg_keys = jax.random.split(jax.random.key(seed), 9)
    velocity = centred(arg_keys[0], (3, NX, NR, NT), 1.0, 6.0, ((1, 32), (3, 16)), jnp.float32)
    mean_flow = jnp.clip(jax.random.uniform(arg_keys[1], (NR,), jnp.float32, 0.5, 1.5), 0.5, 1.5)
    part_x = with_ends(jax.random.randint(arg_keys[2], (N_STREAM, N_AZI, N_AZI, CAP), 0, CX), jax.random.fold_in(arg_keys[2], 1), 0, CX - 1).astype(jnp.int32)
    part_r = with_ends(jax.random.randint(arg_keys[3], (N_STREAM, N_AZI, N_AZI, CAP), 0, CR), jax.random.fold_in(arg_keys[3], 1), 0, CR - 1).astype(jnp.int32)
    part_t = with_ends(jax.random.randint(arg_keys[4], (N_STREAM, N_AZI, N_AZI, CAP), 0, CT), jax.random.fold_in(arg_keys[4], 1), 0, CT - 1).astype(jnp.int32)
    part_vel = centred(arg_keys[5], (N_STREAM, N_AZI, N_AZI, 3, CAP), 1.0, 6.0, ((0, 32), (1, 16)), jnp.float32)
    part_rate = jnp.clip(jnp.exp(math.log(5.0) - 2.3025851 * jax.random.uniform(arg_keys[6], (N_STREAM, N_AZI, N_AZI, CAP), jnp.float32) ** shard_levels(arg_keys[6], (N_STREAM, N_AZI, N_AZI, CAP), ((0, 32), (1, 16)), -0.2, 0.2)), 0.5, 5.0)
    counts = draw_counts(jax.random.fold_in(arg_keys[8], 71), 0)
    return {"velocity": velocity, "mean_flow": mean_flow, "part_x": part_x, "part_r": part_r, "part_t": part_t, "part_vel": part_vel, "part_rate": part_rate, "counts": counts}


def stencil(velocity, mean_flow):
    count_r = velocity.shape[2]
    j_index = jnp.arange(count_r, dtype=jnp.float32)
    radius = 0.5 + 0.5 * (j_index + 0.5) / count_r
    h_term = (0.25 / (count_r * radius))[None, None, :, None]
    k_term = ((0.75 / radius) ** 2)[None, None, :, None]
    x_plus = jnp.roll(velocity, -1, axis=1)
    x_minus = jnp.roll(velocity, 1, axis=1)
    t_plus = jnp.roll(velocity, -1, axis=3)
    t_minus = jnp.roll(velocity, 1, axis=3)
    padded = jnp.pad(velocity, ((0, 0), (0, 0), (1, 1), (0, 0)))
    r_plus = padded[:, :, 2:, :]
    r_minus = padded[:, :, :-2, :]
    lap = (x_plus + x_minus - 2.0 * velocity) + (1.0 + h_term) * r_plus + (1.0 - h_term) * r_minus - 2.0 * velocity
    lap = lap + k_term * (t_plus + t_minus - 2.0 * velocity)
    advect = -0.15 * mean_flow[None, None, :, None] * (x_plus - x_minus)
    return velocity + 0.08 * lap + advect


def reference(velocity, mean_flow, part_x, part_r, part_t, part_vel, part_rate, counts):
    slots = jnp.arange(CAP, dtype=jnp.int32)
    live = (slots[None, None, None, :] < counts[..., None]).astype(jnp.float32)
    rate = part_rate * live
    stream_id = jnp.arange(N_STREAM, dtype=jnp.int32)[:, None, None, None]
    owner_id = jnp.arange(N_AZI, dtype=jnp.int32)[None, None, :, None]
    global_x = stream_id * CX + part_x
    global_t = owner_id * CT + part_t
    flat_index = ((global_x * NR + part_r) * NT + global_t).astype(jnp.int32)
    flat_field = velocity.reshape(3, -1)
    fluid_at = jnp.moveaxis(flat_field[:, flat_index], 0, 3)
    kick = 0.1 * rate[:, :, :, None, :] * (fluid_at - part_vel)
    new_part_vel = part_vel + kick
    pushes = (-0.5 * jnp.moveaxis(kick, 3, 0)).reshape(3, -1)
    deposit = jnp.zeros_like(flat_field).at[:, flat_index.reshape(-1)].add(pushes)
    new_velocity = stencil(velocity, mean_flow) + deposit.reshape(velocity.shape)
    return new_velocity, new_part_vel
```

```python
import functools

import jax
import jax.numpy as jnp
from jax import lax
from jax.experimental import pallas as pl
from jax.experimental.pallas import tpu as pltpu
from jax.sharding import PartitionSpec as P

MESH = pl.DeviceIdType.MESH
F32, BF16, I32 = jnp.float32, jnp.bfloat16, jnp.int32
GROUP = 4


def iota(shape, dim):
    return lax.broadcasted_iota(I32, shape, dim)


def remote(src, dst, send, recv, to):
    return pltpu.make_async_remote_copy(src, dst, send, recv, device_id=to, device_id_type=MESH)


def column(row):
    return jnp.broadcast_to(row, (row.shape[1], row.shape[1])).T


def kernel(sizes, vel, mean, part_x, part_r, part_t, part_vel, part_rate, counts, out_v, out_p,
           field, mean_b, x_b, r_b, t_b, vel_b, rate_b, counts_b, msg, rec, back, home, planes, edge, edge_in,
           turned, hot, push, load_sem, plane_send, plane_recv, rec_send, rec_recv, back_send, back_recv, edge_send, edge_recv):
    ns, na = sizes
    _, _, nr, nt = field.shape
    rows = 2 * nr
    s, a = lax.axis_index("stream"), lax.axis_index("azi")
    right, left = (lax.rem(s + 1, ns), a), (lax.rem(s + ns - 1, ns), a)

    def ahead(i):
        return lax.rem(a + i, na)

    barrier = pltpu.get_barrier_semaphore()
    peers = [right, left] + [(s, ahead(i)) for i in range(1, na)]
    for peer in peers:
        pl.semaphore_signal(barrier, inc=1, device_id=peer, device_id_type=MESH)
    loads = [
        pltpu.make_async_copy(src, dst, load_sem.at[i])
        for i, (src, dst) in enumerate(
            [(part_x, x_b), (part_r, r_b), (part_t, t_b), (part_vel, vel_b), (part_rate, rate_b), (counts, counts_b), (mean, mean_b), (vel, field)]
        )
    ]
    for load in loads:
        load.start()
    for load in loads[:6]:
        load.wait()

    cnt = jnp.where(iota((na, na), 0) == iota((na, na), 1), counts_b[0].astype(F32), 0.0)
    cnt = jnp.sum(cnt, axis=1, keepdims=True)
    live = iota((na, nt), 1).astype(F32) < cnt
    for c in range(3):
        msg[:, c, :] = vel_b[0, 0, c]
    msg[:, 3, :] = jnp.where(live, rate_b[0, 0], 0.0)
    msg[:, 4, :] = (x_b[0, 0] * nr + r_b[0, 0]).astype(F32)
    msg[:, 5, :] = t_b[0, 0].astype(F32)
    msg[:, 6:8, :] = jnp.zeros((na, 2, nt), F32)

    loads[6].wait()
    loads[7].wait()
    pl.semaphore_wait(barrier, len(peers))
    sent = []
    for c in range(3):
        for d, to in ((0, right), (1, left)):
            cp = remote(field.at[c, 1 - d], planes.at[d, c], plane_send.at[d, c], plane_recv.at[d, c], to)
            cp.start()
            sent.append(cp)
    records = [None]
    for i in range(1, na):
        cp = remote(msg.at[ahead(i)], rec.at[i], rec_send.at[i], rec_recv.at[i], (s, ahead(i)))
        cp.start()
        records.append(cp)
    rec[0] = msg[a]

    edge[:, 3:8, :] = jnp.zeros((2, 5, rows), F32)
    for c in range(3):
        for p in range(2):
            for k in range(0, nr, nt):
                at = p * nr + k
                block = field[c, p, pl.ds(k, nt), :].T
                edge[0, c:c + 1, at:at + nt] = block[0:1]
                edge[1, c:c + 1, at:at + nt] = block[nt - 1:nt]
                high = block.astype(BF16)
                turned[c * nt:(c + 1) * nt, at:at + nt] = high
                turned[(3 + c) * nt:(4 + c) * nt, at:at + nt] = (block - high.astype(F32)).astype(BF16)
    for d, to in ((0, (s, ahead(1))), (1, (s, ahead(na - 1)))):
        cp = remote(edge.at[1 - d], edge_in.at[d], edge_send.at[d], edge_recv.at[d], to)
        cp.start()
        sent.append(cp)

    j = iota((nr, nt), 0)
    radius = 0.5 + 0.5 * (j.astype(F32) + 0.5) / nr
    h = 0.25 / (nr * radius)
    k = (0.75 / radius) * (0.75 / radius)
    flow = 0.15 * jnp.concatenate([column(mean_b[i:i + nt].reshape(1, nt)) for i in range(0, nr, nt)], axis=0)
    lane = iota((nr, nt), 1)
    own = 1.0 - 0.32 - 0.16 * k
    outer = jnp.where(j < nr - 1, 0.08 * (1.0 + h), 0.0)
    inner = jnp.where(j > 0, 0.08 * (1.0 - h), 0.0)
    after = jnp.where(lane < nt - 1, 0.08 * k, 0.0)
    before = jnp.where(lane > 0, 0.08 * k, 0.0)
    up, down = 0.08 - flow, 0.08 + flow
    for c in range(3):
        for p in range(2):
            u = field[c, p]
            new = u * own + outer * pltpu.roll(u, nr - 1, 0) + inner * pltpu.roll(u, 1, 0)
            new += after * pltpu.roll(u, nt - 1, 1) + before * pltpu.roll(u, 1, 1)
            out_v[c, p] = new + (up if p == 0 else down) * field[c, 1 - p]

    for g in range(0, na, GROUP):
        for i in range(g, g + GROUP):
            if i:
                records[i].wait_recv()
            row = rec[i, 4:5, :].astype(I32)
            hot[:, i * nt:(i + 1) * nt] = jnp.where(iota((rows, nt), 0) == row, 1.0, 0.0).astype(BF16)
        at = lax.dot_general(turned[...], hot[:, g * nt:(g + GROUP) * nt], (((1,), (0,)), ((), ())), preferred_element_type=F32)
        at = at[:3 * nt] + at[3 * nt:]
        for i in range(g, g + GROUP):
            here = iota((nt, nt), 0) == rec[i, 5:6, :].astype(I32)
            rate = 0.1 * rec[i, 3:4, :]
            for c in range(3):
                fluid = at[c * nt:(c + 1) * nt, (i - g) * nt:(i - g + 1) * nt]
                fluid = jnp.sum(jnp.where(here, fluid, 0.0), axis=0, keepdims=True)
                old = rec[i, c:c + 1, :]
                kick = rate * (fluid - old)
                back[i, c:c + 1, :] = old + kick
                kick = -0.5 * kick
                high = kick.astype(BF16).astype(F32)
                push[0, c * nt:(c + 1) * nt, i * nt:(i + 1) * nt] = jnp.where(here, high, 0.0).astype(BF16)
                push[1, c * nt:(c + 1) * nt, i * nt:(i + 1) * nt] = jnp.where(here, kick - high, 0.0).astype(BF16)
            if i:
                cp = remote(back.at[i], home.at[a], back_send.at[i], back_recv.at[i], (s, ahead(na - i)))
                cp.start()
                sent.append(cp)
            else:
                home[a] = back[0]

    contract = (((1,), (1,)), ((), ()))
    deposit = lax.dot_general(hot[...], push[0], contract, preferred_element_type=F32)
    deposit += lax.dot_general(hot[...], push[1], contract, preferred_element_type=F32)

    for cp in sent[6:8]:
        cp.wait_recv()
    lanes = lax.rem(iota((1, rows), 1), nr).astype(F32)
    radius = 0.5 + 0.5 * (lanes + 0.5) / nr
    k = 0.08 * (0.75 / radius) * (0.75 / radius)
    sides = jnp.concatenate([edge_in[0], edge_in[1]], axis=0) * k
    which, where = iota((16, 3 * nt), 0), iota((16, 3 * nt), 1)
    place = jnp.logical_or(where == which * nt, where == (which - 8) * nt + nt - 1)
    place = jnp.where(jnp.logical_and(place, lax.rem(which, 8) < 3), 1.0, 0.0)
    deposit += lax.dot_general(sides, place, (((0,), (0,)), ((), ())), preferred_element_type=F32, precision=lax.Precision.HIGHEST)

    for c in range(3):
        for p in range(2):
            sent[2 * c + p].wait_recv()
            new = out_v[c, p] + deposit[p * nr:(p + 1) * nr, c * nt:(c + 1) * nt]
            out_v[c, p] = new + (down if p == 0 else up) * planes[p, c]

    for i in range(1, na):
        records[i].wait_send()
    for cp in sent:
        cp.wait_send()
    for cp in sent[8:]:
        cp.wait_recv()
    for c in range(3):
        out_p[0, 0, c] = home[:, c, :]


def body(velocity, mean_flow, part_x, part_r, part_t, part_vel, part_rate, counts):
    ns, na = lax.axis_size("stream"), lax.axis_size("azi")
    _, _, nr, nt = velocity.shape
    rows = 2 * nr
    sem = pltpu.SemaphoreType.DMA
    part_vel = jnp.swapaxes(part_vel, 2, 3)
    inputs = (velocity, mean_flow, part_x, part_r, part_t, part_vel, part_rate, counts)
    inputs = tuple(pltpu.with_memory_space_constraint(x, pltpu.HBM) for x in inputs)
    staged = [pltpu.VMEM(x.shape, x.dtype) for x in inputs]
    new_velocity, new_vel = pl.pallas_call(
        functools.partial(kernel, (ns, na)),
        out_shape=(pltpu.VMEM(velocity.shape, F32), pltpu.VMEM(part_vel.shape, F32)),
        in_specs=[pl.BlockSpec(memory_space=pltpu.HBM)] * 8,
        out_specs=[pl.BlockSpec(memory_space=pltpu.VMEM)] * 2,
        scratch_shapes=staged
        + [
            pltpu.VMEM((na, 8, nt), F32),
            pltpu.VMEM((na, 8, nt), F32),
            pltpu.VMEM((na, 3, nt), F32),
            pltpu.VMEM((na, 3, nt), F32),
            pltpu.VMEM((2, 3, nr, nt), F32),
            pltpu.VMEM((2, 8, rows), F32),
            pltpu.VMEM((2, 8, rows), F32),
            pltpu.VMEM((6 * nt, rows), BF16),
            pltpu.VMEM((rows, na * nt), BF16),
            pltpu.VMEM((2, 3 * nt, na * nt), BF16),
            sem((8,)), sem((2, 3)), sem((2, 3)), sem((na,)), sem((na,)), sem((na,)), sem((na,)), sem((2,)), sem((2,)),
        ],
        compiler_params=pltpu.CompilerParams(collective_id=0, has_side_effects=True, vmem_limit_bytes=48 * 1024 * 1024),
        name="substep",
    )(*inputs)
    return new_velocity, jnp.swapaxes(new_vel, 2, 3)


def solution(mesh):
    in_specs = (
        P(None, "stream", None, "azi"),
        P(),
        P("stream", "azi", None, None),
        P("stream", "azi", None, None),
        P("stream", "azi", None, None),
        P("stream", "azi", None, None, None),
        P("stream", "azi", None, None),
        P("stream", "azi", None),
    )
    out_specs = (P(None, "stream", None, "azi"), P("stream", "azi", None, None, None))
    return jax.shard_map(body, mesh=mesh, in_specs=in_specs, out_specs=out_specs, check_vma=False)
```

```python
import functools

import jax
import jax.numpy as jnp
from jax import lax
from jax.experimental import pallas as pl
from jax.experimental.pallas import tpu as pltpu
from jax.sharding import PartitionSpec as P

MESH = pl.DeviceIdType.MESH
F32, BF16, I32 = jnp.float32, jnp.bfloat16, jnp.int32
GROUP, PARTS = 4, 4


def iota(shape, dim):
    return lax.broadcasted_iota(I32, shape, dim)


def remote(src, dst, send, recv, to):
    return pltpu.make_async_remote_copy(src, dst, send, recv, device_id=to, device_id_type=MESH)


def column(row):
    return jnp.broadcast_to(row, (row.shape[1], row.shape[1])).T


def kernel(sizes, vel, mean, part_x, part_r, part_t, part_vel, part_rate, counts, out_v, out_p,
           field, mean_b, x_b, r_b, t_b, vel_b, rate_b, counts_b, msg, rec, back, home, planes, edge, edge_in,
           turned, hot, push, load_sem, ready, near, go, passing, pass_send, pass_recv, plane_send, plane_recv, rec_send, rec_recv, back_send, back_recv, edge_send, edge_recv):
    ns, na = sizes
    _, _, nr, nt = field.shape
    rows, groups = 2 * nr, na // GROUP
    s, a = lax.axis_index("stream"), lax.axis_index("azi")
    right, left = lax.rem(s + 1, ns), lax.rem(s + ns - 1, ns)
    mine = a // GROUP
    half, part = ns // 2, nr // PARTS
    p, late = lax.rem(s, half), s >= half
    first, last = p == 0, p == half - 1
    over = lax.rem(s + half, ns)
    away = jnp.where(p < half // 2, p, half - 1 - p) // 2
    relay = jnp.logical_and(jnp.where(p < half // 2, p, half - 1 - p) == 2 * away, jnp.logical_and(away > 0, away < PARTS))
    upper = p >= half // 2

    def each(first, last, act):
        def step(i, carry):
            act(i)
            return carry

        lax.fori_loop(first, last, step, 0)

    def signal(sem, to):
        pl.semaphore_signal(sem, inc=1, device_id=to, device_id_type=MESH)

    barrier = pltpu.get_barrier_semaphore()
    each(a + 1, na, lambda i: signal(barrier, (s, i)))
    pl.when(right > s)(lambda: signal(barrier, (right, a)))
    pl.when(left > s)(lambda: signal(barrier, (left, a)))
    for n in range(1, PARTS):
        pl.when(first)(lambda: signal(barrier, (s + 2 * n, a)))
        pl.when(jnp.logical_and(first, s < half))(lambda: signal(barrier, (ns - 1 - 2 * n, a)))
        pl.when(jnp.logical_and(last, s < half))(lambda: signal(barrier, (half + 2 * n, a)))
    end = s - p + half - 1
    pl.when(jnp.logical_and(relay, s < half))(lambda: signal(barrier, (jnp.where(upper, half, ns - 1), a)))
    pl.when(jnp.logical_and(relay, upper))(lambda: signal(barrier, (end, a)))
    loads = [
        pltpu.make_async_copy(src, dst, load_sem.at[i])
        for i, (src, dst) in enumerate(
            [(part_x, x_b), (part_r, r_b), (part_t, t_b), (part_vel, vel_b), (part_rate, rate_b), (counts, counts_b), (mean, mean_b), (vel, field)]
        )
    ]
    for load in loads:
        load.start()
    earlier = a + jnp.where(left < s, 1, 0) + jnp.where(right < s, 1, 0)
    earlier += jnp.where(jnp.logical_and(late, jnp.logical_or(first, last)), PARTS - 1, 0) + jnp.where(last, PARTS - 1, 0)
    earlier += jnp.where(jnp.logical_and(relay, late), 1, 0) + jnp.where(jnp.logical_and(relay, jnp.logical_not(upper)), 1, 0)
    pl.when(earlier > 0)(lambda: pl.semaphore_wait(barrier, earlier))
    pl.when(left < s)(lambda: signal(near.at[0], (left, a)))
    pl.when(right < s)(lambda: signal(near.at[1], (right, a)))
    pl.when(jnp.logical_and(relay, late))(lambda: signal(near.at[jnp.where(upper, 1, 0)], (jnp.where(upper, 0, half - 1), a)))
    for n in range(1, PARTS):
        pl.when(last)(lambda: signal(go.at[0], (s - 2 * n, a)))

    def plane(d, n):
        at = pl.ds(n * part, part)
        to = (left if d else right, a)
        return remote(vel.at[:, 1 - d, at], planes.at[d, :, at], plane_send.at[d, n], plane_recv.at[d, n], to)

    def first_leg(d, n):
        at = pl.ds(n * part, part)
        to = (left - 2 * n if d else right + 2 * n, a)
        return remote(vel.at[:, 1 - d, at], passing, plane_send.at[d, n], pass_recv.at[0], to)

    def second_leg():
        at = pl.ds(pl.multiple_of(away * part, part), part)
        d = jnp.where(upper, 1, 0)
        to = (jnp.where(upper, end, s - p), a)
        return remote(passing, planes.at[d, :, at], pass_send.at[0], plane_recv.at[d, away], to)

    def send_planes(d):
        for n in range(PARTS):
            plane(d, n).start()

    def send_far(d):
        for n in reversed(range(PARTS)):
            (first_leg(d, n) if n else plane(d, n)).start()

    def pass_on():
        pl.when(upper)(lambda: pl.semaphore_wait(go.at[0], 1))
        first_leg(0, 1).wait_recv()
        second_leg().start()

    def record(i, src, dst, send, recv, slot):
        return remote(src.at[i], dst.at[slot], send.at[i], recv.at[slot], (s, i))

    def send_record(i):
        record(i, msg, rec, rec_send, rec_recv, a).start()

    def meet(i):
        pl.semaphore_wait(ready.at[i], 1)
        send_record(i)

    pl.when(jnp.logical_and(last, late))(lambda: send_far(0))
    pl.when(jnp.logical_and(first, late))(lambda: send_far(1))
    pl.when(jnp.logical_not(first))(lambda: send_planes(1))
    each(0, a, lambda i: signal(ready.at[a], (s, i)))

    for load in loads[:6]:
        load.wait()
    cnt = jnp.where(iota((na, na), 0) == iota((na, na), 1), counts_b[0].astype(F32), 0.0)
    cnt = jnp.sum(cnt, axis=1, keepdims=True)
    live = iota((na, nt), 1).astype(F32) < cnt
    for c in range(3):
        msg[:, c, :] = vel_b[0, 0, c]
    msg[:, 3, :] = jnp.where(live, rate_b[0, 0], 0.0)
    msg[:, 4, :] = (x_b[0, 0] * nr + r_b[0, 0]).astype(F32)
    msg[:, 5, :] = t_b[0, 0].astype(F32)
    msg[:, 6:8, :] = jnp.zeros((na, 2, nt), F32)
    each(0, a, send_record)
    each(a + 1, (mine + 1) * GROUP, meet)
    rec[a] = msg[a]

    @pl.when(jnp.logical_not(last))
    def _():
        pl.semaphore_wait(near.at[0], 1)
        send_planes(0)

    loads[6].wait()
    loads[7].wait()
    edge[:, 3:8, :] = jnp.zeros((2, 5, rows), F32)
    for c in range(3):
        for m in range(2):
            for k in range(0, nr, nt):
                at = m * nr + k
                block = field[c, m, pl.ds(k, nt), :].T
                edge[0, c:c + 1, at:at + nt] = block[0:1]
                edge[1, c:c + 1, at:at + nt] = block[nt - 1:nt]
                high = block.astype(BF16)
                turned[c * nt:(c + 1) * nt, at:at + nt] = high
                turned[(3 + c) * nt:(4 + c) * nt, at:at + nt] = (block - high.astype(F32)).astype(BF16)

    j = iota((nr, nt), 0)
    radius = 0.5 + 0.5 * (j.astype(F32) + 0.5) / nr
    h = 0.25 / (nr * radius)
    k = (0.75 / radius) * (0.75 / radius)
    flow = 0.15 * jnp.concatenate([column(mean_b[i:i + nt].reshape(1, nt)) for i in range(0, nr, nt)], axis=0)
    lane = iota((nr, nt), 1)
    own = 1.0 - 0.32 - 0.16 * k
    outer = jnp.where(j < nr - 1, 0.08 * (1.0 + h), 0.0)
    inner = jnp.where(j > 0, 0.08 * (1.0 - h), 0.0)
    after = jnp.where(lane < nt - 1, 0.08 * k, 0.0)
    before = jnp.where(lane > 0, 0.08 * k, 0.0)
    up, down = 0.08 - flow, 0.08 + flow
    for c in range(3):
        for m in range(2):
            u = field[c, m]
            new = u * own + outer * pltpu.roll(u, nr - 1, 0) + inner * pltpu.roll(u, 1, 0)
            new += after * pltpu.roll(u, nt - 1, 1) + before * pltpu.roll(u, 1, 1)
            out_v[c, m] = new + (up if m == 0 else down) * field[c, 1 - m]

    edges = [
        remote(edge.at[1 - d], edge_in.at[d], edge_send.at[d], edge_recv.at[d], (s, lax.rem(a + (1 if d == 0 else na - 1), na)))
        for d in range(2)
    ]
    for q in range(groups):
        later = mine + 1 + q
        pl.when(later < groups)(lambda: each(later * GROUP, (later + 1) * GROUP, meet))
        if q == groups - 2:
            for cp in edges:
                cp.start()
        start = jnp.where(q <= mine, mine - q, q) * GROUP
        for n in range(GROUP):
            i = start + n
            pl.when(i != a)(lambda: record(i, msg, rec, rec_send, rec_recv, i).wait_recv())
            row = rec[i, 4:5, :].astype(I32)
            at = (q * GROUP + n) * nt
            hot[:, at:at + nt] = jnp.where(iota((rows, nt), 0) == row, 1.0, 0.0).astype(BF16)
        at = q * GROUP * nt
        values = lax.dot_general(turned[...], hot[:, at:at + GROUP * nt], (((1,), (0,)), ((), ())), preferred_element_type=F32)
        values = values[:3 * nt] + values[3 * nt:]
        for n in range(GROUP):
            i, at = start + n, (q * GROUP + n) * nt
            here = iota((nt, nt), 0) == rec[i, 5:6, :].astype(I32)
            rate = 0.1 * rec[i, 3:4, :]
            for c in range(3):
                fluid = values[c * nt:(c + 1) * nt, n * nt:(n + 1) * nt]
                fluid = jnp.sum(jnp.where(here, fluid, 0.0), axis=0, keepdims=True)
                old = rec[i, c:c + 1, :]
                kick = rate * (fluid - old)
                back[i, c:c + 1, :] = old + kick
                kick = -0.5 * kick
                high = kick.astype(BF16).astype(F32)
                push[0, c * nt:(c + 1) * nt, at:at + nt] = jnp.where(here, high, 0.0).astype(BF16)
                push[1, c * nt:(c + 1) * nt, at:at + nt] = jnp.where(here, kick - high, 0.0).astype(BF16)
            pl.when(i != a)(lambda: record(i, back, home, back_send, back_recv, a).start())
    home[a] = back[a]

    for d, edge_of in ((0, last), (1, first)):
        @pl.when(jnp.logical_and(edge_of, s < half))
        def _():
            pl.semaphore_wait(near.at[d], PARTS)
            send_far(d)

    pl.when(relay)(pass_on)

    contract = (((1,), (1,)), ((), ()))
    deposit = lax.dot_general(hot[...], push[0], contract, preferred_element_type=F32)
    deposit += lax.dot_general(hot[...], push[1], contract, preferred_element_type=F32)

    for cp in edges:
        cp.wait_recv()
    lanes = lax.rem(iota((1, rows), 1), nr).astype(F32)
    radius = 0.5 + 0.5 * (lanes + 0.5) / nr
    k = 0.08 * (0.75 / radius) * (0.75 / radius)
    sides = jnp.concatenate([edge_in[0], edge_in[1]], axis=0) * k
    which, where = iota((16, 3 * nt), 0), iota((16, 3 * nt), 1)
    place = jnp.logical_or(where == which * nt, where == (which - 8) * nt + nt - 1)
    place = jnp.where(jnp.logical_and(place, lax.rem(which, 8) < 3), 1.0, 0.0)
    deposit += lax.dot_general(sides, place, (((0,), (0,)), ((), ())), preferred_element_type=F32, precision=lax.Precision.HIGHEST)

    for n in range(PARTS):
        for d in range(2):
            plane(d, n).wait_recv()
            for c in range(3):
                lo, hi = n * part, (n + 1) * part
                new = out_v[c, d, lo:hi] + deposit[d * nr + lo:d * nr + hi, c * nt:(c + 1) * nt]
                out_v[c, d, lo:hi] = new + (down if d == 0 else up)[lo:hi] * planes[d, c, lo:hi]

    def settle(i):
        record(i, msg, rec, rec_send, rec_recv, a).wait_send()
        record(i, back, home, back_send, back_recv, a).wait_send()
        record(i, back, home, back_send, back_recv, i).wait_recv()

    each(0, a, settle)
    each(a + 1, na, settle)
    for c in range(3):
        out_p[0, 0, c] = home[:, c, :]
    for d in range(2):
        edges[d].wait_send()
        for n in range(PARTS):
            plane(d, n).wait_send()
    pl.when(relay)(lambda: second_leg().wait_send())


def body(velocity, mean_flow, part_x, part_r, part_t, part_vel, part_rate, counts):
    ns, na = lax.axis_size("stream"), lax.axis_size("azi")
    _, _, nr, nt = velocity.shape
    rows = 2 * nr
    sem = pltpu.SemaphoreType.DMA
    part_vel = jnp.swapaxes(part_vel, 2, 3)
    inputs = (velocity, mean_flow, part_x, part_r, part_t, part_vel, part_rate, counts)
    inputs = tuple(pltpu.with_memory_space_constraint(x, pltpu.HBM) for x in inputs)
    staged = [pltpu.VMEM(x.shape, x.dtype) for x in inputs]
    new_velocity, new_vel = pl.pallas_call(
        functools.partial(kernel, (ns, na)),
        out_shape=(pltpu.VMEM(velocity.shape, F32), pltpu.VMEM(part_vel.shape, F32)),
        in_specs=[pl.BlockSpec(memory_space=pltpu.HBM)] * 8,
        out_specs=[pl.BlockSpec(memory_space=pltpu.VMEM)] * 2,
        scratch_shapes=staged
        + [
            pltpu.VMEM((na, 8, nt), F32),
            pltpu.VMEM((na, 8, nt), F32),
            pltpu.VMEM((na, 3, nt), F32),
            pltpu.VMEM((na, 3, nt), F32),
            pltpu.VMEM((2, 3, nr, nt), F32),
            pltpu.VMEM((2, 8, rows), F32),
            pltpu.VMEM((2, 8, rows), F32),
            pltpu.VMEM((6 * nt, rows), BF16),
            pltpu.VMEM((rows, na * nt), BF16),
            pltpu.VMEM((2, 3 * nt, na * nt), BF16),
            sem((8,)), pltpu.SemaphoreType.REGULAR((na,)), pltpu.SemaphoreType.REGULAR((2,)), pltpu.SemaphoreType.REGULAR((1,)),
            pltpu.VMEM((3, nr // PARTS, nt), F32), sem((1,)), sem((1,)), sem((2, PARTS)), sem((2, PARTS)), sem((na,)), sem((na,)), sem((na,)), sem((na,)), sem((2,)), sem((2,)),
        ],
        compiler_params=pltpu.CompilerParams(collective_id=0, has_side_effects=True, vmem_limit_bytes=48 * 1024 * 1024),
        name="substep",
    )(*inputs)
    return new_velocity, jnp.swapaxes(new_vel, 2, 3)


def solution(mesh):
    in_specs = (
        P(None, "stream", None, "azi"),
        P(),
        P("stream", "azi", None, None),
        P("stream", "azi", None, None),
        P("stream", "azi", None, None),
        P("stream", "azi", None, None, None),
        P("stream", "azi", None, None),
        P("stream", "azi", None),
    )
    out_specs = (P(None, "stream", None, "azi"), P("stream", "azi", None, None, None))
    return jax.shard_map(body, mesh=mesh, in_specs=in_specs, out_specs=out_specs, check_vma=False)
```

```python
import functools

import jax
import jax.numpy as jnp
from jax import lax
from jax.experimental import pallas as pl
from jax.experimental.pallas import tpu as pltpu
from jax.sharding import PartitionSpec as P

MESH = pl.DeviceIdType.MESH
F32, BF16, I32 = jnp.float32, jnp.bfloat16, jnp.int32
GROUP, PARTS, RELAYS = 4, 4, 2


def iota(shape, dim):
    return lax.broadcasted_iota(I32, shape, dim)


def remote(src, dst, send, recv, to):
    return pltpu.make_async_remote_copy(src, dst, send, recv, device_id=to, device_id_type=MESH)


def column(row):
    return jnp.broadcast_to(row, (row.shape[1], row.shape[1])).T


def kernel(sizes, vel, mean, part_x, part_r, part_t, part_vel, part_rate, counts, out_v, out_p,
           field, mean_b, x_b, r_b, t_b, vel_b, rate_b, counts_b, msg, rec, back, home, planes, edge, edge_in,
           turned, hot, push, load_sem, ready, near, go, passing, pass_send, pass_recv, plane_send, plane_recv, rec_send, rec_recv, back_send, back_recv, edge_send, edge_recv):
    ns, na = sizes
    _, _, nr, nt = field.shape
    rows, groups = 2 * nr, na // GROUP
    s, a = lax.axis_index("stream"), lax.axis_index("azi")
    right, left = lax.rem(s + 1, ns), lax.rem(s + ns - 1, ns)
    mine = a // GROUP
    half, part = ns // 2, nr // PARTS
    p, late = lax.rem(s, half), s >= half
    first, last = p == 0, p == half - 1
    over = lax.rem(s + half, ns)
    away = jnp.where(p < half // 2, p, half - 1 - p) // 2
    relay = jnp.logical_and(jnp.where(p < half // 2, p, half - 1 - p) == 2 * away, jnp.logical_and(away > 0, away <= RELAYS))
    upper = p >= half // 2

    def each(first, last, act):
        def step(i, carry):
            act(i)
            return carry

        lax.fori_loop(first, last, step, 0)

    def signal(sem, to):
        pl.semaphore_signal(sem, inc=1, device_id=to, device_id_type=MESH)

    barrier = pltpu.get_barrier_semaphore()
    each(a + 1, na, lambda i: signal(barrier, (s, i)))
    pl.when(right > s)(lambda: signal(barrier, (right, a)))
    pl.when(left > s)(lambda: signal(barrier, (left, a)))
    for n in range(1, RELAYS + 1):
        pl.when(first)(lambda: signal(barrier, (s + 2 * n, a)))
        pl.when(jnp.logical_and(first, s < half))(lambda: signal(barrier, (ns - 1 - 2 * n, a)))
        pl.when(jnp.logical_and(last, s < half))(lambda: signal(barrier, (half + 2 * n, a)))
    end = s - p + half - 1
    pl.when(jnp.logical_and(relay, s < half))(lambda: signal(barrier, (jnp.where(upper, half, ns - 1), a)))
    pl.when(jnp.logical_and(relay, upper))(lambda: signal(barrier, (end, a)))
    loads = [
        pltpu.make_async_copy(src, dst, load_sem.at[i])
        for i, (src, dst) in enumerate(
            [(part_x, x_b), (part_r, r_b), (part_t, t_b), (part_vel, vel_b), (part_rate, rate_b), (counts, counts_b), (mean, mean_b), (vel, field)]
        )
    ]
    for load in loads:
        load.start()
    earlier = a + jnp.where(left < s, 1, 0) + jnp.where(right < s, 1, 0)
    earlier += jnp.where(jnp.logical_and(late, jnp.logical_or(first, last)), RELAYS, 0) + jnp.where(last, RELAYS, 0)
    earlier += jnp.where(jnp.logical_and(relay, late), 1, 0) + jnp.where(jnp.logical_and(relay, jnp.logical_not(upper)), 1, 0)
    pl.when(earlier > 0)(lambda: pl.semaphore_wait(barrier, earlier))
    pl.when(left < s)(lambda: signal(near.at[0], (left, a)))
    pl.when(right < s)(lambda: signal(near.at[1], (right, a)))
    pl.when(jnp.logical_and(relay, late))(lambda: signal(near.at[jnp.where(upper, 1, 0)], (jnp.where(upper, 0, half - 1), a)))
    for n in range(1, RELAYS + 1):
        pl.when(last)(lambda: signal(go.at[0], (s - 2 * n, a)))

    def plane(d, n):
        at = pl.ds(n * part, part)
        to = (left if d else right, a)
        return remote(vel.at[:, 1 - d, at], planes.at[d, :, at], plane_send.at[d, n], plane_recv.at[d, n], to)

    def first_leg(d, n):
        at = pl.ds((PARTS - n) * part, part)
        to = (left - 2 * n if d else right + 2 * n, a)
        return remote(vel.at[:, 1 - d, at], passing, plane_send.at[d, PARTS - n], pass_recv.at[0], to)

    def second_leg():
        n = PARTS - away
        at = pl.ds(pl.multiple_of(n * part, part), part)
        d = jnp.where(upper, 1, 0)
        to = (jnp.where(upper, end, s - p), a)
        return remote(passing, planes.at[d, :, at], pass_send.at[0], plane_recv.at[d, n], to)

    def send_planes(d):
        for n in range(PARTS):
            plane(d, n).start()

    def send_far(d):
        for n in reversed(range(1, RELAYS + 1)):
            first_leg(d, n).start()

    def send_rest(d):
        for n in range(PARTS - RELAYS):
            plane(d, n).start()

    def pass_on():
        pl.when(upper)(lambda: pl.semaphore_wait(go.at[0], 1))
        first_leg(0, 1).wait_recv()
        second_leg().start()

    def record(i, src, dst, send, recv, slot):
        return remote(src.at[i], dst.at[slot], send.at[i], recv.at[slot], (s, i))

    def send_record(i):
        record(i, msg, rec, rec_send, rec_recv, a).start()

    def meet(i):
        pl.semaphore_wait(ready.at[i], 1)
        send_record(i)

    pl.when(jnp.logical_and(last, late))(lambda: send_far(0))
    pl.when(jnp.logical_and(first, late))(lambda: send_far(1))
    each(0, a, lambda i: signal(ready.at[a], (s, i)))

    for load in loads[:6]:
        load.wait()
    cnt = jnp.where(iota((na, na), 0) == iota((na, na), 1), counts_b[0].astype(F32), 0.0)
    cnt = jnp.sum(cnt, axis=1, keepdims=True)
    live = iota((na, nt), 1).astype(F32) < cnt
    for c in range(3):
        msg[:, c, :] = vel_b[0, 0, c]
    msg[:, 3, :] = jnp.where(live, rate_b[0, 0], 0.0)
    msg[:, 4, :] = (x_b[0, 0] * nr + r_b[0, 0]).astype(F32)
    msg[:, 5, :] = t_b[0, 0].astype(F32)
    msg[:, 6:8, :] = jnp.zeros((na, 2, nt), F32)
    each(0, a, send_record)
    pl.when(jnp.logical_and(last, late))(lambda: send_rest(0))
    pl.when(jnp.logical_and(first, late))(lambda: send_rest(1))
    each(a + 1, (mine + 1) * GROUP, meet)
    rec[a] = msg[a]

    def send_near():
        pl.when(jnp.logical_not(first))(lambda: send_planes(1))

        @pl.when(jnp.logical_not(last))
        def _():
            pl.semaphore_wait(near.at[0], 1)
            send_planes(0)


    loads[6].wait()
    loads[7].wait()
    edge[:, 3:8, :] = jnp.zeros((2, 5, rows), F32)
    for c in range(3):
        for m in range(2):
            for k in range(0, nr, nt):
                at = m * nr + k
                block = field[c, m, pl.ds(k, nt), :].T
                edge[0, c:c + 1, at:at + nt] = block[0:1]
                edge[1, c:c + 1, at:at + nt] = block[nt - 1:nt]
                high = block.astype(BF16)
                turned[c * nt:(c + 1) * nt, at:at + nt] = high
                turned[(3 + c) * nt:(4 + c) * nt, at:at + nt] = (block - high.astype(F32)).astype(BF16)

    j = iota((nr, nt), 0)
    radius = 0.5 + 0.5 * (j.astype(F32) + 0.5) / nr
    h = 0.25 / (nr * radius)
    k = (0.75 / radius) * (0.75 / radius)
    flow = 0.15 * jnp.concatenate([column(mean_b[i:i + nt].reshape(1, nt)) for i in range(0, nr, nt)], axis=0)
    lane = iota((nr, nt), 1)
    own = 1.0 - 0.32 - 0.16 * k
    outer = jnp.where(j < nr - 1, 0.08 * (1.0 + h), 0.0)
    inner = jnp.where(j > 0, 0.08 * (1.0 - h), 0.0)
    after = jnp.where(lane < nt - 1, 0.08 * k, 0.0)
    before = jnp.where(lane > 0, 0.08 * k, 0.0)
    up, down = 0.08 - flow, 0.08 + flow
    for c in range(3):
        for m in range(2):
            u = field[c, m]
            new = u * own + outer * pltpu.roll(u, nr - 1, 0) + inner * pltpu.roll(u, 1, 0)
            new += after * pltpu.roll(u, nt - 1, 1) + before * pltpu.roll(u, 1, 1)
            out_v[c, m] = new + (up if m == 0 else down) * field[c, 1 - m]

    edges = [
        remote(edge.at[1 - d], edge_in.at[d], edge_send.at[d], edge_recv.at[d], (s, lax.rem(a + (1 if d == 0 else na - 1), na)))
        for d in range(2)
    ]
    send_near()
    for q in range(groups):
        later = mine + 1 + q
        pl.when(later < groups)(lambda: each(later * GROUP, (later + 1) * GROUP, meet))
        if q == groups - 2:
            for cp in edges:
                cp.start()
        if q == groups - 1:
            for d, edge_of in ((0, last), (1, first)):
                @pl.when(jnp.logical_and(edge_of, s < half))
                def _():
                    pl.semaphore_wait(near.at[d], RELAYS + 1)
                    send_far(d)
        start = jnp.where(q <= mine, mine - q, q) * GROUP
        for n in range(GROUP):
            i = start + n
            pl.when(i != a)(lambda: record(i, msg, rec, rec_send, rec_recv, i).wait_recv())
            row = rec[i, 4:5, :].astype(I32)
            at = (q * GROUP + n) * nt
            hot[:, at:at + nt] = jnp.where(iota((rows, nt), 0) == row, 1.0, 0.0).astype(BF16)
        at = q * GROUP * nt
        values = lax.dot_general(turned[...], hot[:, at:at + GROUP * nt], (((1,), (0,)), ((), ())), preferred_element_type=F32)
        values = values[:3 * nt] + values[3 * nt:]
        for n in range(GROUP):
            i, at = start + n, (q * GROUP + n) * nt
            here = iota((nt, nt), 0) == rec[i, 5:6, :].astype(I32)
            rate = 0.1 * rec[i, 3:4, :]
            for c in range(3):
                fluid = values[c * nt:(c + 1) * nt, n * nt:(n + 1) * nt]
                fluid = jnp.sum(jnp.where(here, fluid, 0.0), axis=0, keepdims=True)
                old = rec[i, c:c + 1, :]
                kick = rate * (fluid - old)
                back[i, c:c + 1, :] = old + kick
                kick = -0.5 * kick
                high = kick.astype(BF16).astype(F32)
                push[0, c * nt:(c + 1) * nt, at:at + nt] = jnp.where(here, high, 0.0).astype(BF16)
                push[1, c * nt:(c + 1) * nt, at:at + nt] = jnp.where(here, kick - high, 0.0).astype(BF16)
            pl.when(i != a)(lambda: record(i, back, home, back_send, back_recv, a).start())
    home[a] = back[a]


    contract = (((1,), (1,)), ((), ()))
    deposit = lax.dot_general(hot[...], push[0], contract, preferred_element_type=F32)
    deposit += lax.dot_general(hot[...], push[1], contract, preferred_element_type=F32)

    pl.when(relay)(pass_on)
    pl.when(jnp.logical_and(last, s < half))(lambda: send_rest(0))
    pl.when(jnp.logical_and(first, s < half))(lambda: send_rest(1))
    for cp in edges:
        cp.wait_recv()
    lanes = lax.rem(iota((1, rows), 1), nr).astype(F32)
    radius = 0.5 + 0.5 * (lanes + 0.5) / nr
    k = 0.08 * (0.75 / radius) * (0.75 / radius)
    sides = jnp.concatenate([edge_in[0], edge_in[1]], axis=0) * k
    which, where = iota((16, 3 * nt), 0), iota((16, 3 * nt), 1)
    place = jnp.logical_or(where == which * nt, where == (which - 8) * nt + nt - 1)
    place = jnp.where(jnp.logical_and(place, lax.rem(which, 8) < 3), 1.0, 0.0)
    deposit += lax.dot_general(sides, place, (((0,), (0,)), ((), ())), preferred_element_type=F32, precision=lax.Precision.HIGHEST)

    for n in range(PARTS):
        for d in range(2):
            plane(d, n).wait_recv()
            for c in range(3):
                lo, hi = n * part, (n + 1) * part
                new = out_v[c, d, lo:hi] + deposit[d * nr + lo:d * nr + hi, c * nt:(c + 1) * nt]
                out_v[c, d, lo:hi] = new + (down if d == 0 else up)[lo:hi] * planes[d, c, lo:hi]

    def settle(i):
        record(i, msg, rec, rec_send, rec_recv, a).wait_send()
        record(i, back, home, back_send, back_recv, a).wait_send()
        record(i, back, home, back_send, back_recv, i).wait_recv()

    each(0, a, settle)
    each(a + 1, na, settle)
    for c in range(3):
        out_p[0, 0, c] = home[:, c, :]
    for d in range(2):
        edges[d].wait_send()
        for n in range(PARTS):
            plane(d, n).wait_send()
    pl.when(relay)(lambda: second_leg().wait_send())


def store(velocity, part_vel, out_v, out_p, sems):
    copies = [pltpu.make_async_copy(velocity.at[c], out_v.at[c], sems.at[c]) for c in range(3)]
    copies.append(pltpu.make_async_copy(part_vel, out_p, sems.at[3]))
    for copy in copies:
        copy.start()
    for copy in copies:
        copy.wait()


def body(velocity, mean_flow, part_x, part_r, part_t, part_vel, part_rate, counts):
    ns, na = lax.axis_size("stream"), lax.axis_size("azi")
    _, _, nr, nt = velocity.shape
    rows = 2 * nr
    sem = pltpu.SemaphoreType.DMA
    part_vel = jnp.swapaxes(part_vel, 2, 3)
    inputs = (velocity, mean_flow, part_x, part_r, part_t, part_vel, part_rate, counts)
    inputs = tuple(pltpu.with_memory_space_constraint(x, pltpu.HBM) for x in inputs)
    staged = [pltpu.VMEM(x.shape, x.dtype) for x in inputs]
    new_velocity, new_vel = pl.pallas_call(
        functools.partial(kernel, (ns, na)),
        out_shape=(pltpu.VMEM(velocity.shape, F32), pltpu.VMEM(part_vel.shape, F32)),
        in_specs=[pl.BlockSpec(memory_space=pltpu.HBM)] * 8,
        out_specs=[pl.BlockSpec(memory_space=pltpu.VMEM)] * 2,
        scratch_shapes=staged
        + [
            pltpu.VMEM((na, 8, nt), F32),
            pltpu.VMEM((na, 8, nt), F32),
            pltpu.VMEM((na, 3, nt), F32),
            pltpu.VMEM((na, 3, nt), F32),
            pltpu.VMEM((2, 3, nr, nt), F32),
            pltpu.VMEM((2, 8, rows), F32),
            pltpu.VMEM((2, 8, rows), F32),
            pltpu.VMEM((6 * nt, rows), BF16),
            pltpu.VMEM((rows, na * nt), BF16),
            pltpu.VMEM((2, 3 * nt, na * nt), BF16),
            sem((8,)), pltpu.SemaphoreType.REGULAR((na,)), pltpu.SemaphoreType.REGULAR((2,)), pltpu.SemaphoreType.REGULAR((1,)),
            pltpu.VMEM((3, nr // PARTS, nt), F32), sem((1,)), sem((1,)), sem((2, PARTS)), sem((2, PARTS)), sem((na,)), sem((na,)), sem((na,)), sem((na,)), sem((2,)), sem((2,)),
        ],
        compiler_params=pltpu.CompilerParams(collective_id=0, has_side_effects=True, vmem_limit_bytes=48 * 1024 * 1024),
        name="substep",
    )(*inputs)
    done = tuple(pltpu.with_memory_space_constraint(x, pltpu.VMEM) for x in (new_velocity, new_vel))
    new_velocity, new_vel = pl.pallas_call(
        store,
        out_shape=tuple(pltpu.HBM(x.shape, x.dtype) for x in done),
        in_specs=[pl.BlockSpec(memory_space=pltpu.VMEM)] * 2,
        out_specs=[pl.BlockSpec(memory_space=pltpu.HBM)] * 2,
        scratch_shapes=[sem((4,))],
        name="store",
    )(*done)
    return new_velocity, jnp.swapaxes(new_vel, 2, 3)


def solution(mesh):
    in_specs = (
        P(None, "stream", None, "azi"),
        P(),
        P("stream", "azi", None, None),
        P("stream", "azi", None, None),
        P("stream", "azi", None, None),
        P("stream", "azi", None, None, None),
        P("stream", "azi", None, None),
        P("stream", "azi", None),
    )
    out_specs = (P(None, "stream", None, "azi"), P("stream", "azi", None, None, None))
    return jax.shard_map(body, mesh=mesh, in_specs=in_specs, out_specs=out_specs, check_vma=False)
```

```python
import functools

import jax
import jax.numpy as jnp
from jax import lax
from jax.experimental import pallas as pl
from jax.experimental.pallas import tpu as pltpu
from jax.sharding import PartitionSpec as P

MESH = pl.DeviceIdType.MESH
F32, BF16, I32 = jnp.float32, jnp.bfloat16, jnp.int32
GROUP, PARTS, RELAYS = 4, 4, 2


def iota(shape, dim):
    return lax.broadcasted_iota(I32, shape, dim)


def remote(src, dst, send, recv, to):
    return pltpu.make_async_remote_copy(src, dst, send, recv, device_id=to, device_id_type=MESH)


def column(row):
    return jnp.broadcast_to(row, (row.shape[1], row.shape[1])).T


def kernel(sizes, vel, mean, part_x, part_r, part_t, part_vel, part_rate, counts, out_v, out_p,
           field, mean_b, x_b, r_b, t_b, vel_b, rate_b, counts_b, msg, rec, back, home, planes, edge, edge_in,
           turned, hot, push, load_sem, ready, near, passing, pass_send, pass_recv, plane_send, plane_recv, rec_send, rec_recv, back_send, back_recv, edge_send, edge_recv):
    ns, na = sizes
    _, _, nr, nt = field.shape
    rows, groups = 2 * nr, na // GROUP
    s, a = lax.axis_index("stream"), lax.axis_index("azi")
    right, left = lax.rem(s + 1, ns), lax.rem(s + ns - 1, ns)
    half, part = ns // 2, nr // PARTS
    p, late = lax.rem(s, half), s >= half
    first, last = p == 0, p == half - 1
    over = lax.rem(s + half, ns)
    away = jnp.where(p < half // 2, p, half - 1 - p) // 2
    relay = jnp.logical_and(jnp.where(p < half // 2, p, half - 1 - p) == 2 * away, jnp.logical_and(away > 0, away <= RELAYS))
    upper = p >= half // 2

    shift = jnp.where(s == 0, 1, 0)
    mine = lax.rem(a + na - shift, na) // GROUP

    def peer(i):
        return lax.rem(i + shift, na)

    def rank(t):
        q = lax.rem(t, half)
        return (t // half) * ns + jnp.where(q < half // 2, 2 * q, 2 * (half - 1 - q) + 1)

    order = lax.rem(a + na - shift, na)
    left_first, right_first = rank(left) < rank(s), rank(right) < rank(s)

    def each(first, last, act):
        def step(i, carry):
            act(i)
            return carry

        lax.fori_loop(first, last, step, 0)

    def signal(sem, to):
        pl.semaphore_signal(sem, inc=1, device_id=to, device_id_type=MESH)

    barrier = pltpu.get_barrier_semaphore()
    each(order + 1, na, lambda i: signal(barrier, (s, peer(i))))
    pl.when(jnp.logical_not(right_first))(lambda: signal(barrier, (right, a)))
    pl.when(jnp.logical_not(left_first))(lambda: signal(barrier, (left, a)))
    for n in range(1, RELAYS + 1):
        pl.when(first)(lambda: signal(barrier, (s + 2 * n, a)))
        pl.when(last)(lambda: signal(barrier, (s - 2 * n, a)))
        pl.when(jnp.logical_and(first, s < half))(lambda: signal(barrier, (ns - 1 - 2 * n, a)))
        pl.when(jnp.logical_and(last, s < half))(lambda: signal(barrier, (half + 2 * n, a)))
    end = s - p + half - 1
    pl.when(jnp.logical_and(relay, s < half))(lambda: signal(barrier, (jnp.where(upper, half, ns - 1), a)))
    loads = [
        pltpu.make_async_copy(src, dst, load_sem.at[i])
        for i, (src, dst) in enumerate(
            [(part_x, x_b), (part_r, r_b), (part_t, t_b), (part_vel, vel_b), (part_rate, rate_b), (counts, counts_b), (mean, mean_b), (vel, field)]
        )
    ]
    for load in loads:
        load.start()
    earlier = order + jnp.where(left_first, 1, 0) + jnp.where(right_first, 1, 0)
    earlier += jnp.where(jnp.logical_and(late, jnp.logical_or(first, last)), RELAYS, 0)
    earlier += jnp.where(jnp.logical_and(relay, late), 1, 0) + jnp.where(relay, 1, 0)
    pl.when(earlier > 0)(lambda: pl.semaphore_wait(barrier, earlier))
    pl.when(left_first)(lambda: signal(near.at[0], (left, a)))
    pl.when(right_first)(lambda: signal(near.at[1], (right, a)))
    pl.when(jnp.logical_and(relay, late))(lambda: signal(near.at[jnp.where(upper, 1, 0)], (jnp.where(upper, 0, half - 1), a)))

    def plane(d, n):
        at = pl.ds(n * part, part)
        to = (left if d else right, a)
        return remote(vel.at[:, 1 - d, at], planes.at[d, :, at], plane_send.at[d, n], plane_recv.at[d, n], to)

    def first_leg(d, n):
        at = pl.ds((PARTS - n) * part, part)
        to = (left - 2 * n if d else right + 2 * n, a)
        return remote(vel.at[:, 1 - d, at], passing, plane_send.at[d, PARTS - n], pass_recv.at[0], to)

    def second_leg():
        n = PARTS - away
        at = pl.ds(pl.multiple_of(n * part, part), part)
        d = jnp.where(upper, 1, 0)
        to = (jnp.where(upper, end, s - p), a)
        return remote(passing, planes.at[d, :, at], pass_send.at[0], plane_recv.at[d, n], to)

    def send_planes(d):
        for n in range(PARTS):
            plane(d, n).start()

    def send_far(d):
        for n in reversed(range(1, RELAYS + 1)):
            first_leg(d, n).start()

    def send_rest(d):
        for n in range(PARTS - RELAYS):
            plane(d, n).start()

    def pass_on():
        first_leg(0, 1).wait_recv()
        second_leg().start()

    def record(i, src, dst, send, recv, slot):
        count = 6 if src is msg else 3
        at = pl.ds(0, count)
        return remote(src.at[i, at], dst.at[slot, at], send.at[i], recv.at[slot], (s, i))

    def send_record(i):
        record(i, msg, rec, rec_send, rec_recv, a).start()

    def meet(i):
        pl.semaphore_wait(ready.at[i], 1)
        send_record(i)

    pl.when(jnp.logical_and(last, late))(lambda: send_far(0))
    pl.when(jnp.logical_and(first, late))(lambda: send_far(1))
    pl.when(jnp.logical_and(last, late))(lambda: send_rest(0))
    pl.when(jnp.logical_and(first, late))(lambda: send_rest(1))
    each(0, order, lambda i: signal(ready.at[a], (s, peer(i))))

    for load in loads[:6]:
        load.wait()
    cnt = jnp.where(iota((na, na), 0) == iota((na, na), 1), counts_b[0].astype(F32), 0.0)
    cnt = jnp.sum(cnt, axis=1, keepdims=True)
    live = iota((na, nt), 1).astype(F32) < cnt
    for c in range(3):
        msg[:, c, :] = vel_b[0, 0, c]
    msg[:, 3, :] = jnp.where(live, rate_b[0, 0], 0.0)
    msg[:, 4, :] = (x_b[0, 0] * nr + r_b[0, 0]).astype(F32)
    msg[:, 5, :] = t_b[0, 0].astype(F32)
    each(0, order, lambda i: send_record(peer(i)))
    each(order + 1, (mine + 1) * GROUP, lambda i: meet(peer(i)))
    rec[a] = msg[a]

    def send_near():
        for d, far, ahead in ((1, first, left_first), (0, last, right_first)):
            pl.when(jnp.logical_not(jnp.logical_or(far, ahead)))(lambda: pl.semaphore_wait(near.at[d], 1))
            pl.when(jnp.logical_not(far))(lambda: send_planes(d))


    loads[6].wait()
    loads[7].wait()
    edge[:, 3:8, :] = jnp.zeros((2, 5, rows), F32)
    for c in range(3):
        for m in range(2):
            for k in range(0, nr, nt):
                at = m * nr + k
                block = field[c, m, pl.ds(k, nt), :].T
                edge[0, c:c + 1, at:at + nt] = block[0:1]
                edge[1, c:c + 1, at:at + nt] = block[nt - 1:nt]
                high = block.astype(BF16)
                turned[c * nt:(c + 1) * nt, at:at + nt] = high
                turned[(3 + c) * nt:(4 + c) * nt, at:at + nt] = (block - high.astype(F32)).astype(BF16)

    j = iota((nr, nt), 0)
    radius = 0.5 + 0.5 * (j.astype(F32) + 0.5) / nr
    h = 0.25 / (nr * radius)
    k = (0.75 / radius) * (0.75 / radius)
    flow = 0.15 * jnp.concatenate([column(mean_b[i:i + nt].reshape(1, nt)) for i in range(0, nr, nt)], axis=0)
    lane = iota((nr, nt), 1)
    own = 1.0 - 0.32 - 0.16 * k
    outer = jnp.where(j < nr - 1, 0.08 * (1.0 + h), 0.0)
    inner = jnp.where(j > 0, 0.08 * (1.0 - h), 0.0)
    after = jnp.where(lane < nt - 1, 0.08 * k, 0.0)
    before = jnp.where(lane > 0, 0.08 * k, 0.0)
    up, down = 0.08 - flow, 0.08 + flow
    for c in range(3):
        for m in range(2):
            u = field[c, m]
            new = u * own + outer * pltpu.roll(u, nr - 1, 0) + inner * pltpu.roll(u, 1, 0)
            new += after * pltpu.roll(u, nt - 1, 1) + before * pltpu.roll(u, 1, 1)
            out_v[c, m] = new + (up if m == 0 else down) * field[c, 1 - m]

    edges = [
        remote(edge.at[1 - d], edge_in.at[d], edge_send.at[d], edge_recv.at[d], (s, lax.rem(a + (1 if d == 0 else na - 1), na)))
        for d in range(2)
    ]
    send_near()
    for q in range(groups):
        later = mine + 1 + q
        pl.when(later < groups)(lambda: each(later * GROUP, (later + 1) * GROUP, lambda i: meet(peer(i))))
        if q == groups - 2:
            for cp in edges:
                cp.start()
        if q == groups - 2:
            for d, edge_of in ((0, last), (1, first)):
                @pl.when(jnp.logical_and(edge_of, s < half))
                def _():
                    pl.semaphore_wait(near.at[d], RELAYS + 1)
                    send_far(d)
                    send_rest(d)
        start = jnp.where(q <= mine, mine - q, q) * GROUP
        for n in range(GROUP):
            i = peer(start + n)
            pl.when(i != a)(lambda: record(i, msg, rec, rec_send, rec_recv, i).wait_recv())
            row = rec[i, 4:5, :].astype(I32)
            at = (q * GROUP + n) * nt
            hot[:, at:at + nt] = jnp.where(iota((rows, nt), 0) == row, 1.0, 0.0).astype(BF16)
        at = q * GROUP * nt
        values = lax.dot_general(turned[...], hot[:, at:at + GROUP * nt], (((1,), (0,)), ((), ())), preferred_element_type=F32)
        values = values[:3 * nt] + values[3 * nt:]
        for n in range(GROUP):
            i, at = peer(start + n), (q * GROUP + n) * nt
            here = iota((nt, nt), 0) == rec[i, 5:6, :].astype(I32)
            rate = 0.1 * rec[i, 3:4, :]
            for c in range(3):
                fluid = values[c * nt:(c + 1) * nt, n * nt:(n + 1) * nt]
                fluid = jnp.sum(jnp.where(here, fluid, 0.0), axis=0, keepdims=True)
                old = rec[i, c:c + 1, :]
                kick = rate * (fluid - old)
                back[i, c:c + 1, :] = old + kick
                kick = -0.5 * kick
                high = kick.astype(BF16).astype(F32)
                push[0, c * nt:(c + 1) * nt, at:at + nt] = jnp.where(here, high, 0.0).astype(BF16)
                push[1, c * nt:(c + 1) * nt, at:at + nt] = jnp.where(here, kick - high, 0.0).astype(BF16)
            pl.when(i != a)(lambda: record(i, back, home, back_send, back_recv, a).start())
    home[a] = back[a]
    pl.when(jnp.logical_and(relay, late))(pass_on)


    contract = (((1,), (1,)), ((), ()))
    deposit = lax.dot_general(hot[...], push[0], contract, preferred_element_type=F32)
    deposit += lax.dot_general(hot[...], push[1], contract, preferred_element_type=F32)

    pl.when(jnp.logical_and(relay, jnp.logical_not(late)))(pass_on)
    for cp in edges:
        cp.wait_recv()
    lanes = lax.rem(iota((1, rows), 1), nr).astype(F32)
    radius = 0.5 + 0.5 * (lanes + 0.5) / nr
    k = 0.08 * (0.75 / radius) * (0.75 / radius)
    sides = jnp.concatenate([edge_in[0], edge_in[1]], axis=0) * k
    which, where = iota((16, 3 * nt), 0), iota((16, 3 * nt), 1)
    place = jnp.logical_or(where == which * nt, where == (which - 8) * nt + nt - 1)
    place = jnp.where(jnp.logical_and(place, lax.rem(which, 8) < 3), 1.0, 0.0)
    deposit += lax.dot_general(sides, place, (((0,), (0,)), ((), ())), preferred_element_type=F32, precision=lax.Precision.HIGHEST)

    def settle(i):
        record(i, msg, rec, rec_send, rec_recv, a).wait_send()
        record(i, back, home, back_send, back_recv, a).wait_send()
        record(i, back, home, back_send, back_recv, i).wait_recv()

    each(0, a, settle)
    each(a + 1, na, settle)
    for c in range(3):
        out_p[0, 0, c] = home[:, c, :]
    for n in range(PARTS):
        for d in range(2):
            plane(d, n).wait_recv()
            for c in range(3):
                lo, hi = n * part, (n + 1) * part
                new = out_v[c, d, lo:hi] + deposit[d * nr + lo:d * nr + hi, c * nt:(c + 1) * nt]
                out_v[c, d, lo:hi] = new + (down if d == 0 else up)[lo:hi] * planes[d, c, lo:hi]

    for d in range(2):
        edges[d].wait_send()
        for n in range(PARTS):
            plane(d, n).wait_send()
    pl.when(relay)(lambda: second_leg().wait_send())


def store(velocity, part_vel, out_v, out_p, sems):
    copies = [pltpu.make_async_copy(velocity.at[c], out_v.at[c], sems.at[c]) for c in range(3)]
    copies.append(pltpu.make_async_copy(part_vel, out_p, sems.at[3]))
    for copy in copies:
        copy.start()
    for copy in copies:
        copy.wait()


def body(velocity, mean_flow, part_x, part_r, part_t, part_vel, part_rate, counts):
    ns, na = lax.axis_size("stream"), lax.axis_size("azi")
    _, _, nr, nt = velocity.shape
    rows = 2 * nr
    sem = pltpu.SemaphoreType.DMA
    part_vel = jnp.swapaxes(part_vel, 2, 3)
    inputs = (velocity, mean_flow, part_x, part_r, part_t, part_vel, part_rate, counts)
    inputs = tuple(pltpu.with_memory_space_constraint(x, pltpu.HBM) for x in inputs)
    staged = [pltpu.VMEM(x.shape, x.dtype) for x in inputs]
    new_velocity, new_vel = pl.pallas_call(
        functools.partial(kernel, (ns, na)),
        out_shape=(pltpu.VMEM(velocity.shape, F32), pltpu.VMEM(part_vel.shape, F32)),
        in_specs=[pl.BlockSpec(memory_space=pltpu.HBM)] * 8,
        out_specs=[pl.BlockSpec(memory_space=pltpu.VMEM)] * 2,
        scratch_shapes=staged
        + [
            pltpu.VMEM((na, 8, nt), F32),
            pltpu.VMEM((na, 8, nt), F32),
            pltpu.VMEM((na, 3, nt), F32),
            pltpu.VMEM((na, 3, nt), F32),
            pltpu.VMEM((2, 3, nr, nt), F32),
            pltpu.VMEM((2, 8, rows), F32),
            pltpu.VMEM((2, 8, rows), F32),
            pltpu.VMEM((6 * nt, rows), BF16),
            pltpu.VMEM((rows, na * nt), BF16),
            pltpu.VMEM((2, 3 * nt, na * nt), BF16),
            sem((8,)), pltpu.SemaphoreType.REGULAR((na,)), pltpu.SemaphoreType.REGULAR((2,)),
            pltpu.VMEM((3, nr // PARTS, nt), F32), sem((1,)), sem((1,)), sem((2, PARTS)), sem((2, PARTS)), sem((na,)), sem((na,)), sem((na,)), sem((na,)), sem((2,)), sem((2,)),
        ],
        compiler_params=pltpu.CompilerParams(collective_id=0, has_side_effects=True, vmem_limit_bytes=48 * 1024 * 1024),
        name="substep",
    )(*inputs)
    done = tuple(pltpu.with_memory_space_constraint(x, pltpu.VMEM) for x in (new_velocity, new_vel))
    new_velocity, new_vel = pl.pallas_call(
        store,
        out_shape=tuple(pltpu.HBM(x.shape, x.dtype) for x in done),
        in_specs=[pl.BlockSpec(memory_space=pltpu.VMEM)] * 2,
        out_specs=[pl.BlockSpec(memory_space=pltpu.HBM)] * 2,
        scratch_shapes=[sem((4,))],
        name="store",
    )(*done)
    return new_velocity, jnp.swapaxes(new_vel, 2, 3)


def solution(mesh):
    in_specs = (
        P(None, "stream", None, "azi"),
        P(),
        P("stream", "azi", None, None),
        P("stream", "azi", None, None),
        P("stream", "azi", None, None),
        P("stream", "azi", None, None, None),
        P("stream", "azi", None, None),
        P("stream", "azi", None),
    )
    out_specs = (P(None, "stream", None, "azi"), P("stream", "azi", None, None, None))
    return jax.shard_map(body, mesh=mesh, in_specs=in_specs, out_specs=out_specs, check_vma=False)
```

```python
import functools

import jax
import jax.numpy as jnp
from jax import lax
from jax.experimental import pallas as pl
from jax.experimental.pallas import tpu as pltpu
from jax.sharding import PartitionSpec as P

MESH = pl.DeviceIdType.MESH
F32, BF16, I32 = jnp.float32, jnp.bfloat16, jnp.int32
GROUP, PARTS, RELAYS = 4, 4, 2


def iota(shape, dim):
    return lax.broadcasted_iota(I32, shape, dim)


def remote(src, dst, send, recv, to):
    return pltpu.make_async_remote_copy(src, dst, send, recv, device_id=to, device_id_type=MESH)


def column(row):
    return jnp.broadcast_to(row, (row.shape[1], row.shape[1])).T


def kernel(sizes, vel, mean, part_x, part_r, part_t, part_vel, part_rate, counts, out_v, out_p,
           field, mean_b, x_b, r_b, t_b, vel_b, rate_b, counts_b, msg, rec, back, home, planes, edge, edge_in,
           turned, hot, push, load_sem, ready, near, passing, pass_send, pass_recv, plane_send, plane_recv, rec_send, rec_recv, back_send, back_recv, edge_send, edge_recv):
    ns, na = sizes
    _, _, nr, nt = field.shape
    rows, groups = 2 * nr, na // GROUP
    s, a = lax.axis_index("stream"), lax.axis_index("azi")
    right, left = lax.rem(s + 1, ns), lax.rem(s + ns - 1, ns)
    half, part = ns // 2, nr // PARTS
    p, late = lax.rem(s, half), s >= half
    first, last = p == 0, p == half - 1
    over = lax.rem(s + half, ns)
    away = jnp.where(p < half // 2, p, half - 1 - p) // 2
    relay = jnp.logical_and(jnp.where(p < half // 2, p, half - 1 - p) == 2 * away, jnp.logical_and(away > 0, away <= RELAYS))
    upper = p >= half // 2

    shift = jnp.where(s == 0, 1, 0)
    mine = lax.rem(a + na - shift, na) // GROUP

    def peer(i):
        return lax.rem(i + shift, na)

    def rank(t):
        q = lax.rem(t, half)
        return (t // half) * ns + jnp.where(q < half // 2, 2 * q, 2 * (half - 1 - q) + 1)

    order = lax.rem(a + na - shift, na)
    left_first, right_first = rank(left) < rank(s), rank(right) < rank(s)

    def each(first, last, act):
        def step(i, carry):
            act(i)
            return carry

        lax.fori_loop(first, last, step, 0)

    def signal(sem, to):
        pl.semaphore_signal(sem, inc=1, device_id=to, device_id_type=MESH)

    barrier = pltpu.get_barrier_semaphore()
    each(order + 1, na, lambda i: signal(barrier, (s, peer(i))))
    pl.when(jnp.logical_not(right_first))(lambda: signal(barrier, (right, a)))
    pl.when(jnp.logical_not(left_first))(lambda: signal(barrier, (left, a)))
    for n in range(1, RELAYS + 1):
        pl.when(first)(lambda: signal(barrier, (s + 2 * n, a)))
        pl.when(last)(lambda: signal(barrier, (s - 2 * n, a)))
        pl.when(jnp.logical_and(first, s < half))(lambda: signal(barrier, (ns - 1 - 2 * n, a)))
        pl.when(jnp.logical_and(last, s < half))(lambda: signal(barrier, (half + 2 * n, a)))
    end = s - p + half - 1
    pl.when(jnp.logical_and(relay, s < half))(lambda: signal(barrier, (jnp.where(upper, half, ns - 1), a)))
    loads = [
        pltpu.make_async_copy(src, dst, load_sem.at[i])
        for i, (src, dst) in enumerate(
            [(part_x, x_b), (part_r, r_b), (part_t, t_b), (part_vel, vel_b), (part_rate, rate_b), (counts, counts_b), (mean, mean_b), (vel, field)]
        )
    ]
    for load in loads:
        load.start()
    earlier = order + jnp.where(left_first, 1, 0) + jnp.where(right_first, 1, 0)
    earlier += jnp.where(jnp.logical_and(late, jnp.logical_or(first, last)), RELAYS, 0)
    earlier += jnp.where(jnp.logical_and(relay, late), 1, 0) + jnp.where(relay, 1, 0)
    pl.when(earlier > 0)(lambda: pl.semaphore_wait(barrier, earlier))
    pl.when(left_first)(lambda: signal(near.at[0], (left, a)))
    pl.when(right_first)(lambda: signal(near.at[1], (right, a)))
    pl.when(jnp.logical_and(relay, late))(lambda: signal(near.at[jnp.where(upper, 1, 0)], (jnp.where(upper, 0, half - 1), a)))

    def plane(d, n):
        at = pl.ds(n * part, part)
        to = (left if d else right, a)
        return remote(vel.at[:, 1 - d, at], planes.at[d, :, at], plane_send.at[d, n], plane_recv.at[d, n], to)

    def first_leg(d, n):
        at = pl.ds((PARTS - n) * part, part)
        to = (left - 2 * n if d else right + 2 * n, a)
        return remote(vel.at[:, 1 - d, at], passing, plane_send.at[d, PARTS - n], pass_recv.at[0], to)

    def second_leg():
        n = PARTS - away
        at = pl.ds(pl.multiple_of(n * part, part), part)
        d = jnp.where(upper, 1, 0)
        to = (jnp.where(upper, end, s - p), a)
        return remote(passing, planes.at[d, :, at], pass_send.at[0], plane_recv.at[d, n], to)

    def send_planes(d):
        for n in range(PARTS):
            plane(d, n).start()

    def send_far(d):
        for n in reversed(range(1, RELAYS + 1)):
            first_leg(d, n).start()

    def send_rest(d):
        for n in range(PARTS - RELAYS):
            plane(d, n).start()

    def pass_on():
        first_leg(0, 1).wait_recv()
        second_leg().start()

    def record(i, src, dst, send, recv, slot):
        count = 6 if src is msg else 3
        at = pl.ds(0, count)
        return remote(src.at[i, at], dst.at[slot, at], send.at[i], recv.at[slot], (s, i))

    def send_record(i):
        record(i, msg, rec, rec_send, rec_recv, a).start()

    def meet(i):
        pl.semaphore_wait(ready.at[i], 1)
        send_record(i)

    pl.when(jnp.logical_and(last, late))(lambda: send_far(0))
    pl.when(jnp.logical_and(first, late))(lambda: send_far(1))
    pl.when(jnp.logical_and(last, late))(lambda: send_rest(0))
    pl.when(jnp.logical_and(first, late))(lambda: send_rest(1))
    each(0, order, lambda i: signal(ready.at[a], (s, peer(i))))

    for load in loads[:6]:
        load.wait()
    cnt = jnp.where(iota((na, na), 0) == iota((na, na), 1), counts_b[0].astype(F32), 0.0)
    cnt = jnp.sum(cnt, axis=1, keepdims=True)
    live = iota((na, nt), 1).astype(F32) < cnt
    for c in range(3):
        msg[:, c, :] = vel_b[0, 0, c]
    msg[:, 3, :] = jnp.where(live, rate_b[0, 0], 0.0)
    msg[:, 4, :] = (x_b[0, 0] * nr + r_b[0, 0]).astype(F32)
    msg[:, 5, :] = t_b[0, 0].astype(F32)
    each(0, order, lambda i: send_record(peer(i)))
    each(order + 1, (mine + 1) * GROUP, lambda i: meet(peer(i)))
    rec[a] = msg[a]

    def send_near():
        for d, far, ahead in ((1, first, left_first), (0, last, right_first)):
            pl.when(jnp.logical_not(jnp.logical_or(far, ahead)))(lambda: pl.semaphore_wait(near.at[d], 1))
            pl.when(jnp.logical_not(far))(lambda: send_planes(d))


    loads[6].wait()
    loads[7].wait()
    edge[:, 3:8, :] = jnp.zeros((2, 5, rows), F32)
    for c in range(3):
        for m in range(2):
            for k in range(0, nr, nt):
                at = m * nr + k
                block = field[c, m, pl.ds(k, nt), :].T
                edge[0, c:c + 1, at:at + nt] = block[0:1]
                edge[1, c:c + 1, at:at + nt] = block[nt - 1:nt]
                high = block.astype(BF16)
                turned[c * nt:(c + 1) * nt, at:at + nt] = high
                turned[(3 + c) * nt:(4 + c) * nt, at:at + nt] = (block - high.astype(F32)).astype(BF16)

    j = iota((nr, nt), 0)
    radius = 0.5 + 0.5 * (j.astype(F32) + 0.5) / nr
    h = 0.25 / (nr * radius)
    k = (0.75 / radius) * (0.75 / radius)
    flow = 0.15 * jnp.concatenate([column(mean_b[i:i + nt].reshape(1, nt)) for i in range(0, nr, nt)], axis=0)
    lane = iota((nr, nt), 1)
    own = 1.0 - 0.32 - 0.16 * k
    outer = jnp.where(j < nr - 1, 0.08 * (1.0 + h), 0.0)
    inner = jnp.where(j > 0, 0.08 * (1.0 - h), 0.0)
    after = jnp.where(lane < nt - 1, 0.08 * k, 0.0)
    before = jnp.where(lane > 0, 0.08 * k, 0.0)
    up, down = 0.08 - flow, 0.08 + flow
    for c in range(3):
        for m in range(2):
            u = field[c, m]
            new = u * own + outer * pltpu.roll(u, nr - 1, 0) + inner * pltpu.roll(u, 1, 0)
            new += after * pltpu.roll(u, nt - 1, 1) + before * pltpu.roll(u, 1, 1)
            out_v[c, m] = new + (up if m == 0 else down) * field[c, 1 - m]

    edges = [
        remote(edge.at[1 - d], edge_in.at[d], edge_send.at[d], edge_recv.at[d], (s, lax.rem(a + (1 if d == 0 else na - 1), na)))
        for d in range(2)
    ]
    for q in range(groups):
        later = mine + 1 + q
        pl.when(later < groups)(lambda: each(later * GROUP, (later + 1) * GROUP, lambda i: meet(peer(i))))
        if q == groups - 2:
            for cp in edges:
                cp.start()
        if q == groups - 2:
            for d, edge_of in ((0, last), (1, first)):
                @pl.when(jnp.logical_and(edge_of, s < half))
                def _():
                    pl.semaphore_wait(near.at[d], RELAYS + 1)
                    send_far(d)
                    send_rest(d)
        if q == 1:
            send_near()
        start = jnp.where(q <= mine, mine - q, q) * GROUP
        for n in range(GROUP):
            i = peer(start + n)
            pl.when(i != a)(lambda: record(i, msg, rec, rec_send, rec_recv, i).wait_recv())
            row = rec[i, 4:5, :].astype(I32)
            at = (q * GROUP + n) * nt
            hot[:, at:at + nt] = jnp.where(iota((rows, nt), 0) == row, 1.0, 0.0).astype(BF16)
        at = q * GROUP * nt
        values = lax.dot_general(turned[...], hot[:, at:at + GROUP * nt], (((1,), (0,)), ((), ())), preferred_element_type=F32)
        values = values[:3 * nt] + values[3 * nt:]
        for n in range(GROUP):
            i, at = peer(start + n), (q * GROUP + n) * nt
            here = iota((nt, nt), 0) == rec[i, 5:6, :].astype(I32)
            rate = 0.1 * rec[i, 3:4, :]
            for c in range(3):
                fluid = values[c * nt:(c + 1) * nt, n * nt:(n + 1) * nt]
                fluid = jnp.sum(jnp.where(here, fluid, 0.0), axis=0, keepdims=True)
                old = rec[i, c:c + 1, :]
                kick = rate * (fluid - old)
                back[i, c:c + 1, :] = old + kick
                kick = -0.5 * kick
                high = kick.astype(BF16).astype(F32)
                push[0, c * nt:(c + 1) * nt, at:at + nt] = jnp.where(here, high, 0.0).astype(BF16)
                push[1, c * nt:(c + 1) * nt, at:at + nt] = jnp.where(here, kick - high, 0.0).astype(BF16)
            pl.when(i != a)(lambda: record(i, back, home, back_send, back_recv, a).start())
    home[a] = back[a]
    pl.when(jnp.logical_and(relay, late))(pass_on)


    contract = (((1,), (1,)), ((), ()))
    deposit = lax.dot_general(hot[...], push[0], contract, preferred_element_type=F32)
    deposit += lax.dot_general(hot[...], push[1], contract, preferred_element_type=F32)

    pl.when(jnp.logical_and(relay, jnp.logical_not(late)))(pass_on)
    for cp in edges:
        cp.wait_recv()
    lanes = lax.rem(iota((1, rows), 1), nr).astype(F32)
    radius = 0.5 + 0.5 * (lanes + 0.5) / nr
    k = 0.08 * (0.75 / radius) * (0.75 / radius)
    sides = jnp.concatenate([edge_in[0], edge_in[1]], axis=0) * k
    which, where = iota((16, 3 * nt), 0), iota((16, 3 * nt), 1)
    place = jnp.logical_or(where == which * nt, where == (which - 8) * nt + nt - 1)
    place = jnp.where(jnp.logical_and(place, lax.rem(which, 8) < 3), 1.0, 0.0)
    deposit += lax.dot_general(sides, place, (((0,), (0,)), ((), ())), preferred_element_type=F32, precision=lax.Precision.HIGHEST)

    def settle(i):
        record(i, msg, rec, rec_send, rec_recv, a).wait_send()
        record(i, back, home, back_send, back_recv, a).wait_send()
        record(i, back, home, back_send, back_recv, i).wait_recv()

    each(0, a, settle)
    each(a + 1, na, settle)
    for c in range(3):
        out_p[0, 0, c] = home[:, c, :]
    for n in range(PARTS):
        for d in range(2):
            plane(d, n).wait_recv()
            for c in range(3):
                lo, hi = n * part, (n + 1) * part
                new = out_v[c, d, lo:hi] + deposit[d * nr + lo:d * nr + hi, c * nt:(c + 1) * nt]
                out_v[c, d, lo:hi] = new + (down if d == 0 else up)[lo:hi] * planes[d, c, lo:hi]

    for d in range(2):
        edges[d].wait_send()
        for n in range(PARTS):
            plane(d, n).wait_send()
    pl.when(relay)(lambda: second_leg().wait_send())


def store(velocity, part_vel, out_v, out_p, sems):
    copies = [pltpu.make_async_copy(velocity.at[i // 2, i % 2], out_v.at[i // 2, i % 2], sems.at[i]) for i in range(6)]
    copies.append(pltpu.make_async_copy(part_vel, out_p, sems.at[6]))
    for copy in copies:
        copy.start()
    for copy in copies:
        copy.wait()


def body(velocity, mean_flow, part_x, part_r, part_t, part_vel, part_rate, counts):
    ns, na = lax.axis_size("stream"), lax.axis_size("azi")
    _, _, nr, nt = velocity.shape
    rows = 2 * nr
    sem = pltpu.SemaphoreType.DMA
    part_vel = jnp.swapaxes(part_vel, 2, 3)
    inputs = (velocity, mean_flow, part_x, part_r, part_t, part_vel, part_rate, counts)
    inputs = tuple(pltpu.with_memory_space_constraint(x, pltpu.HBM) for x in inputs)
    staged = [pltpu.VMEM(x.shape, x.dtype) for x in inputs]
    new_velocity, new_vel = pl.pallas_call(
        functools.partial(kernel, (ns, na)),
        out_shape=(pltpu.VMEM(velocity.shape, F32), pltpu.VMEM(part_vel.shape, F32)),
        in_specs=[pl.BlockSpec(memory_space=pltpu.HBM)] * 8,
        out_specs=[pl.BlockSpec(memory_space=pltpu.VMEM)] * 2,
        scratch_shapes=staged
        + [
            pltpu.VMEM((na, 8, nt), F32),
            pltpu.VMEM((na, 8, nt), F32),
            pltpu.VMEM((na, 3, nt), F32),
            pltpu.VMEM((na, 3, nt), F32),
            pltpu.VMEM((2, 3, nr, nt), F32),
            pltpu.VMEM((2, 8, rows), F32),
            pltpu.VMEM((2, 8, rows), F32),
            pltpu.VMEM((6 * nt, rows), BF16),
            pltpu.VMEM((rows, na * nt), BF16),
            pltpu.VMEM((2, 3 * nt, na * nt), BF16),
            sem((8,)), pltpu.SemaphoreType.REGULAR((na,)), pltpu.SemaphoreType.REGULAR((2,)),
            pltpu.VMEM((3, nr // PARTS, nt), F32), sem((1,)), sem((1,)), sem((2, PARTS)), sem((2, PARTS)), sem((na,)), sem((na,)), sem((na,)), sem((na,)), sem((2,)), sem((2,)),
        ],
        compiler_params=pltpu.CompilerParams(collective_id=0, has_side_effects=True, vmem_limit_bytes=48 * 1024 * 1024),
        name="substep",
    )(*inputs)
    done = tuple(pltpu.with_memory_space_constraint(x, pltpu.VMEM) for x in (new_velocity, new_vel))
    new_velocity, new_vel = pl.pallas_call(
        store,
        out_shape=tuple(pltpu.HBM(x.shape, x.dtype) for x in done),
        in_specs=[pl.BlockSpec(memory_space=pltpu.VMEM)] * 2,
        out_specs=[pl.BlockSpec(memory_space=pltpu.HBM)] * 2,
        scratch_shapes=[sem((7,))],
        name="store",
    )(*done)
    return new_velocity, jnp.swapaxes(new_vel, 2, 3)


def solution(mesh):
    in_specs = (
        P(None, "stream", None, "azi"),
        P(),
        P("stream", "azi", None, None),
        P("stream", "azi", None, None),
        P("stream", "azi", None, None),
        P("stream", "azi", None, None, None),
        P("stream", "azi", None, None),
        P("stream", "azi", None),
    )
    out_specs = (P(None, "stream", None, "azi"), P("stream", "azi", None, None, None))
    return jax.shard_map(body, mesh=mesh, in_specs=in_specs, out_specs=out_specs, check_vma=False)
```

```python
import functools

import jax
import jax.numpy as jnp
from jax import lax
from jax.experimental import pallas as pl
from jax.experimental.pallas import tpu as pltpu
from jax.sharding import PartitionSpec as P

MESH = pl.DeviceIdType.MESH
F32, BF16, I32 = jnp.float32, jnp.bfloat16, jnp.int32
GROUP, PARTS, RELAYS = 4, 8, 2


def iota(shape, dim):
    return lax.broadcasted_iota(I32, shape, dim)


def remote(src, dst, send, recv, to):
    return pltpu.make_async_remote_copy(src, dst, send, recv, device_id=to, device_id_type=MESH)


def column(row):
    return jnp.broadcast_to(row, (row.shape[1], row.shape[1])).T


def kernel(sizes, vel, mean, part_x, part_r, part_t, part_vel, part_rate, counts, out_v, out_p,
           field, mean_b, x_b, r_b, t_b, vel_b, rate_b, counts_b, msg, rec, back, home, planes, edge, edge_in,
           turned, hot, push, load_sem, ready, near, passing, pass_send, pass_recv, plane_send, plane_recv, rec_send, rec_recv, back_send, back_recv, edge_send, edge_recv):
    ns, na = sizes
    _, _, nr, nt = field.shape
    rows, groups = 2 * nr, na // GROUP
    s, a = lax.axis_index("stream"), lax.axis_index("azi")
    right, left = lax.rem(s + 1, ns), lax.rem(s + ns - 1, ns)
    half, part = ns // 2, nr // PARTS
    p, late = lax.rem(s, half), s >= half
    first, last = p == 0, p == half - 1
    over = lax.rem(s + half, ns)
    away = jnp.where(p < half // 2, p, half - 1 - p) // 2
    relay = jnp.logical_and(jnp.where(p < half // 2, p, half - 1 - p) == 2 * away, jnp.logical_and(away > 0, away <= RELAYS))
    upper = p >= half // 2

    shift = jnp.where(s == 0, 1, 0)
    mine = lax.rem(a + na - shift, na) // GROUP

    def peer(i):
        return lax.rem(i + shift, na)

    def rank(t):
        q = lax.rem(t, half)
        return (t // half) * ns + jnp.where(q < half // 2, 2 * q, 2 * (half - 1 - q) + 1)

    order = lax.rem(a + na - shift, na)
    left_first, right_first = rank(left) < rank(s), rank(right) < rank(s)

    def each(first, last, act):
        def step(i, carry):
            act(i)
            return carry

        lax.fori_loop(first, last, step, 0)

    def signal(sem, to):
        pl.semaphore_signal(sem, inc=1, device_id=to, device_id_type=MESH)

    barrier = pltpu.get_barrier_semaphore()
    each(order + 1, na, lambda i: signal(barrier, (s, peer(i))))
    pl.when(jnp.logical_not(right_first))(lambda: signal(barrier, (right, a)))
    pl.when(jnp.logical_not(left_first))(lambda: signal(barrier, (left, a)))
    for n in range(1, RELAYS + 1):
        pl.when(first)(lambda: signal(barrier, (s + 2 * n, a)))
        pl.when(last)(lambda: signal(barrier, (s - 2 * n, a)))
        pl.when(jnp.logical_and(first, s < half))(lambda: signal(barrier, (ns - 1 - 2 * n, a)))
        pl.when(jnp.logical_and(last, s < half))(lambda: signal(barrier, (half + 2 * n, a)))
    end = s - p + half - 1
    pl.when(jnp.logical_and(relay, s < half))(lambda: signal(barrier, (jnp.where(upper, half, ns - 1), a)))
    loads = [
        pltpu.make_async_copy(src, dst, load_sem.at[i])
        for i, (src, dst) in enumerate(
            [(part_x, x_b), (part_r, r_b), (part_t, t_b), (part_vel, vel_b), (part_rate, rate_b), (counts, counts_b), (mean, mean_b), (vel, field)]
        )
    ]
    for load in loads:
        load.start()
    earlier = order + jnp.where(left_first, 1, 0) + jnp.where(right_first, 1, 0)
    earlier += jnp.where(jnp.logical_and(late, jnp.logical_or(first, last)), RELAYS, 0)
    earlier += jnp.where(jnp.logical_and(relay, late), 1, 0) + jnp.where(relay, 1, 0)
    pl.when(earlier > 0)(lambda: pl.semaphore_wait(barrier, earlier))
    pl.when(left_first)(lambda: signal(near.at[0], (left, a)))
    pl.when(right_first)(lambda: signal(near.at[1], (right, a)))
    pl.when(jnp.logical_and(relay, late))(lambda: signal(near.at[jnp.where(upper, 1, 0)], (jnp.where(upper, 0, half - 1), a)))

    def plane(d, n):
        at = pl.ds(n * part, part)
        to = (left if d else right, a)
        return remote(vel.at[:, 1 - d, at], planes.at[d, :, at], plane_send.at[d, n], plane_recv.at[d, n], to)

    def first_leg(d, n, m):
        k = PARTS - 2 * n + m
        at = pl.ds(k * part, part)
        to = (left - 2 * n if d else right + 2 * n, a)
        return remote(vel.at[:, 1 - d, at], passing.at[m], plane_send.at[d, k], pass_recv.at[m], to)

    def second_leg(m):
        k = PARTS - 2 * away + m
        at = pl.ds(pl.multiple_of(k * part, part), part)
        d = jnp.where(upper, 1, 0)
        to = (jnp.where(upper, end, s - p), a)
        return remote(passing.at[m], planes.at[d, :, at], pass_send.at[m], plane_recv.at[d, k], to)

    def send_planes(d):
        for n in range(PARTS):
            plane(d, n).start()

    def send_far(d):
        for m in range(2):
            for n in reversed(range(1, RELAYS + 1)):
                first_leg(d, n, m).start()

    def send_rest(d):
        for n in range(PARTS - 2 * RELAYS):
            plane(d, n).start()

    def pass_on():
        for m in range(2):
            first_leg(0, 1, m).wait_recv()
            second_leg(m).start()

    def record(i, src, dst, send, recv, slot):
        count = 6 if src is msg else 3
        at = pl.ds(0, count)
        return remote(src.at[i, at], dst.at[slot, at], send.at[i], recv.at[slot], (s, i))

    def send_record(i):
        record(i, msg, rec, rec_send, rec_recv, a).start()

    def meet(i):
        pl.semaphore_wait(ready.at[i], 1)
        send_record(i)

    pl.when(jnp.logical_and(last, late))(lambda: send_far(0))
    pl.when(jnp.logical_and(first, late))(lambda: send_far(1))
    pl.when(jnp.logical_and(last, late))(lambda: send_rest(0))
    pl.when(jnp.logical_and(first, late))(lambda: send_rest(1))
    each(0, order, lambda i: signal(ready.at[a], (s, peer(i))))

    for load in loads[:6]:
        load.wait()
    cnt = jnp.where(iota((na, na), 0) == iota((na, na), 1), counts_b[0].astype(F32), 0.0)
    cnt = jnp.sum(cnt, axis=1, keepdims=True)
    live = iota((na, nt), 1).astype(F32) < cnt
    for c in range(3):
        msg[:, c, :] = vel_b[0, 0, c]
    msg[:, 3, :] = jnp.where(live, rate_b[0, 0], 0.0)
    msg[:, 4, :] = (x_b[0, 0] * nr + r_b[0, 0]).astype(F32)
    msg[:, 5, :] = t_b[0, 0].astype(F32)
    each(0, order, lambda i: send_record(peer(i)))
    each(order + 1, (mine + 1) * GROUP, lambda i: meet(peer(i)))
    rec[a] = msg[a]

    def send_near():
        for d, far, ahead in ((1, first, left_first), (0, last, right_first)):
            pl.when(jnp.logical_not(jnp.logical_or(far, ahead)))(lambda: pl.semaphore_wait(near.at[d], 1))
            pl.when(jnp.logical_not(far))(lambda: send_planes(d))


    loads[6].wait()
    loads[7].wait()
    edge[:, 3:8, :] = jnp.zeros((2, 5, rows), F32)
    for c in range(3):
        for m in range(2):
            for k in range(0, nr, nt):
                at = m * nr + k
                block = field[c, m, pl.ds(k, nt), :].T
                edge[0, c:c + 1, at:at + nt] = block[0:1]
                edge[1, c:c + 1, at:at + nt] = block[nt - 1:nt]
                high = block.astype(BF16)
                turned[c * nt:(c + 1) * nt, at:at + nt] = high
                turned[(3 + c) * nt:(4 + c) * nt, at:at + nt] = (block - high.astype(F32)).astype(BF16)

    j = iota((nr, nt), 0)
    radius = 0.5 + 0.5 * (j.astype(F32) + 0.5) / nr
    h = 0.25 / (nr * radius)
    k = (0.75 / radius) * (0.75 / radius)
    flow = 0.15 * jnp.concatenate([column(mean_b[i:i + nt].reshape(1, nt)) for i in range(0, nr, nt)], axis=0)
    lane = iota((nr, nt), 1)
    own = 1.0 - 0.32 - 0.16 * k
    outer = jnp.where(j < nr - 1, 0.08 * (1.0 + h), 0.0)
    inner = jnp.where(j > 0, 0.08 * (1.0 - h), 0.0)
    after = jnp.where(lane < nt - 1, 0.08 * k, 0.0)
    before = jnp.where(lane > 0, 0.08 * k, 0.0)
    up, down = 0.08 - flow, 0.08 + flow
    for c in range(3):
        for m in range(2):
            u = field[c, m]
            new = u * own + outer * pltpu.roll(u, nr - 1, 0) + inner * pltpu.roll(u, 1, 0)
            new += after * pltpu.roll(u, nt - 1, 1) + before * pltpu.roll(u, 1, 1)
            out_v[c, m] = new + (up if m == 0 else down) * field[c, 1 - m]

    edges = [
        remote(edge.at[1 - d], edge_in.at[d], edge_send.at[d], edge_recv.at[d], (s, lax.rem(a + (1 if d == 0 else na - 1), na)))
        for d in range(2)
    ]
    for q in range(groups):
        later = mine + 1 + q
        pl.when(later < groups)(lambda: each(later * GROUP, (later + 1) * GROUP, lambda i: meet(peer(i))))
        if q == groups - 2:
            for cp in edges:
                cp.start()
        if q == groups - 2:
            for d, edge_of in ((0, last), (1, first)):
                @pl.when(jnp.logical_and(edge_of, s < half))
                def _():
                    pl.semaphore_wait(near.at[d], RELAYS + 1)
                    send_far(d)
                    send_rest(d)
        if q == 1:
            send_near()
        start = jnp.where(q <= mine, mine - q, q) * GROUP
        for n in range(GROUP):
            i = peer(start + n)
            pl.when(i != a)(lambda: record(i, msg, rec, rec_send, rec_recv, i).wait_recv())
            row = rec[i, 4:5, :].astype(I32)
            at = (q * GROUP + n) * nt
            hot[:, at:at + nt] = jnp.where(iota((rows, nt), 0) == row, 1.0, 0.0).astype(BF16)
        at = q * GROUP * nt
        values = lax.dot_general(turned[...], hot[:, at:at + GROUP * nt], (((1,), (0,)), ((), ())), preferred_element_type=F32)
        values = values[:3 * nt] + values[3 * nt:]
        for n in range(GROUP):
            i, at = peer(start + n), (q * GROUP + n) * nt
            here = iota((nt, nt), 0) == rec[i, 5:6, :].astype(I32)
            rate = 0.1 * rec[i, 3:4, :]
            for c in range(3):
                fluid = values[c * nt:(c + 1) * nt, n * nt:(n + 1) * nt]
                fluid = jnp.sum(jnp.where(here, fluid, 0.0), axis=0, keepdims=True)
                old = rec[i, c:c + 1, :]
                kick = rate * (fluid - old)
                back[i, c:c + 1, :] = old + kick
                kick = -0.5 * kick
                high = kick.astype(BF16).astype(F32)
                push[0, c * nt:(c + 1) * nt, at:at + nt] = jnp.where(here, high, 0.0).astype(BF16)
                push[1, c * nt:(c + 1) * nt, at:at + nt] = jnp.where(here, kick - high, 0.0).astype(BF16)
            pl.when(i != a)(lambda: record(i, back, home, back_send, back_recv, a).start())
    home[a] = back[a]
    pl.when(jnp.logical_and(relay, late))(pass_on)


    contract = (((1,), (1,)), ((), ()))
    deposit = lax.dot_general(hot[...], push[0], contract, preferred_element_type=F32)
    deposit += lax.dot_general(hot[...], push[1], contract, preferred_element_type=F32)

    pl.when(jnp.logical_and(relay, jnp.logical_not(late)))(pass_on)
    for cp in edges:
        cp.wait_recv()
    lanes = lax.rem(iota((1, rows), 1), nr).astype(F32)
    radius = 0.5 + 0.5 * (lanes + 0.5) / nr
    k = 0.08 * (0.75 / radius) * (0.75 / radius)
    sides = jnp.concatenate([edge_in[0], edge_in[1]], axis=0) * k
    which, where = iota((16, 3 * nt), 0), iota((16, 3 * nt), 1)
    place = jnp.logical_or(where == which * nt, where == (which - 8) * nt + nt - 1)
    place = jnp.where(jnp.logical_and(place, lax.rem(which, 8) < 3), 1.0, 0.0)
    deposit += lax.dot_general(sides, place, (((0,), (0,)), ((), ())), preferred_element_type=F32, precision=lax.Precision.HIGHEST)

    def settle(i):
        record(i, msg, rec, rec_send, rec_recv, a).wait_send()
        record(i, back, home, back_send, back_recv, a).wait_send()
        record(i, back, home, back_send, back_recv, i).wait_recv()

    each(0, a, settle)
    each(a + 1, na, settle)
    for c in range(3):
        out_p[0, 0, c] = home[:, c, :]
    for n in range(PARTS):
        for d in range(2):
            plane(d, n).wait_recv()
            for c in range(3):
                lo, hi = n * part, (n + 1) * part
                new = out_v[c, d, lo:hi] + deposit[d * nr + lo:d * nr + hi, c * nt:(c + 1) * nt]
                out_v[c, d, lo:hi] = new + (down if d == 0 else up)[lo:hi] * planes[d, c, lo:hi]

    for d in range(2):
        edges[d].wait_send()
        for n in range(PARTS):
            plane(d, n).wait_send()
    for m in range(2):
        pl.when(relay)(lambda: second_leg(m).wait_send())


def store(velocity, part_vel, out_v, out_p, sems):
    copies = [pltpu.make_async_copy(velocity.at[i // 2, i % 2], out_v.at[i // 2, i % 2], sems.at[i]) for i in range(6)]
    copies.append(pltpu.make_async_copy(part_vel, out_p, sems.at[6]))
    for copy in copies:
        copy.start()
    for copy in copies:
        copy.wait()


def body(velocity, mean_flow, part_x, part_r, part_t, part_vel, part_rate, counts):
    ns, na = lax.axis_size("stream"), lax.axis_size("azi")
    _, _, nr, nt = velocity.shape
    rows = 2 * nr
    sem = pltpu.SemaphoreType.DMA
    part_vel = jnp.swapaxes(part_vel, 2, 3)
    inputs = (velocity, mean_flow, part_x, part_r, part_t, part_vel, part_rate, counts)
    inputs = tuple(pltpu.with_memory_space_constraint(x, pltpu.HBM) for x in inputs)
    staged = [pltpu.VMEM(x.shape, x.dtype) for x in inputs]
    new_velocity, new_vel = pl.pallas_call(
        functools.partial(kernel, (ns, na)),
        out_shape=(pltpu.VMEM(velocity.shape, F32), pltpu.VMEM(part_vel.shape, F32)),
        in_specs=[pl.BlockSpec(memory_space=pltpu.HBM)] * 8,
        out_specs=[pl.BlockSpec(memory_space=pltpu.VMEM)] * 2,
        scratch_shapes=staged
        + [
            pltpu.VMEM((na, 8, nt), F32),
            pltpu.VMEM((na, 8, nt), F32),
            pltpu.VMEM((na, 3, nt), F32),
            pltpu.VMEM((na, 3, nt), F32),
            pltpu.VMEM((2, 3, nr, nt), F32),
            pltpu.VMEM((2, 8, rows), F32),
            pltpu.VMEM((2, 8, rows), F32),
            pltpu.VMEM((6 * nt, rows), BF16),
            pltpu.VMEM((rows, na * nt), BF16),
            pltpu.VMEM((2, 3 * nt, na * nt), BF16),
            sem((8,)), pltpu.SemaphoreType.REGULAR((na,)), pltpu.SemaphoreType.REGULAR((2,)),
            pltpu.VMEM((2, 3, nr // PARTS, nt), F32), sem((2,)), sem((2,)), sem((2, PARTS)), sem((2, PARTS)), sem((na,)), sem((na,)), sem((na,)), sem((na,)), sem((2,)), sem((2,)),
        ],
        compiler_params=pltpu.CompilerParams(collective_id=0, has_side_effects=True, vmem_limit_bytes=48 * 1024 * 1024),
        name="substep",
    )(*inputs)
    done = tuple(pltpu.with_memory_space_constraint(x, pltpu.VMEM) for x in (new_velocity, new_vel))
    new_velocity, new_vel = pl.pallas_call(
        store,
        out_shape=tuple(pltpu.HBM(x.shape, x.dtype) for x in done),
        in_specs=[pl.BlockSpec(memory_space=pltpu.VMEM)] * 2,
        out_specs=[pl.BlockSpec(memory_space=pltpu.HBM)] * 2,
        scratch_shapes=[sem((7,))],
        name="store",
    )(*done)
    return new_velocity, jnp.swapaxes(new_vel, 2, 3)


def solution(mesh):
    in_specs = (
        P(None, "stream", None, "azi"),
        P(),
        P("stream", "azi", None, None),
        P("stream", "azi", None, None),
        P("stream", "azi", None, None),
        P("stream", "azi", None, None, None),
        P("stream", "azi", None, None),
        P("stream", "azi", None),
    )
    out_specs = (P(None, "stream", None, "azi"), P("stream", "azi", None, None, None))
    return jax.shard_map(body, mesh=mesh, in_specs=in_specs, out_specs=out_specs, check_vma=False)
```
